256 devices in a mesh: row: 16 (over z_lo, y), col: 16 (over z_hi, x, core).
Axes of the slice: x: 4, y: 4, z: 8 (z_hi: 2, z_lo: 4; z = z_hi * 4 + z_lo), core: 2. Of those that a mesh axis runs over, the one named last changes fastest.
Arguments:
- amplitudes_right: float32 [8, 16384], P(None, ('row', 'col')), may hold values from -5 to 5
- amplitudes_left: float32 [8, 16384], P(None, ('row', 'col')), may hold values from -7 to 7
- previous_right: float32 [8, 16384], P(None, ('row', 'col')), may hold values from -6 to 6
- previous_left: float32 [8, 16384], P(None, ('row', 'col')), may hold values from -6 to 6
- coupling: float32 [2, 8], replicated, may hold values from 0.2 to 1
- ladder: bfloat16 [16384, 16384], P('row', 'col'), may hold values from -1 to 5
Outputs:
- next_right: float32 [8, 16384], P(None, ('row', 'col'))
- next_left: float32 [8, 16384], P(None, ('row', 'col'))
- coefficients: float32 [3, 8], replicated
The draws below stay inside these ranges and needn't reach their ends.
All inputs are finite; a program needn't handle non-finite values.
Results may differ from the reference program's by a relative error of at most 0.003.
Values may be sent and summed in bfloat16 or wider, within the bound.
No kernel may reach another device: no remote copies, remote signals or barrier semaphores. Data moves between devices by JAX's collectives and lax.ppermute only.
A program may use at most 64 MiB of HBM per device.

```python
import jax
import jax.numpy as jnp
from jax import lax

COLS = 8
PAIRS = 16384


def shared_base(key):
    return jnp.clip(jax.random.normal(jax.random.fold_in(key, 11), (COLS, PAIRS), jnp.float32), -5.0, 5.0)


def draw_amplitudes_right(key, part):
    base = shared_base(key)
    return base


def draw_amplitudes_left(key, part):
    base = shared_base(key)
    key = jax.random.fold_in(key, 2)
    key_mix, key_noise = jax.random.split(key)
    mixing = jax.random.uniform(key_mix, (COLS, 1), jnp.float32, -0.6, 0.6)
    noise = jnp.clip(jax.random.normal(key_noise, (COLS, PAIRS), jnp.float32), -5.0, 5.0)
    return mixing * base + 0.8 * noise


def draw_ladder(key, part):
    key = jax.random.fold_in(key, 3)
    key_off, key_diag = jax.random.split(key)
    spread = jnp.clip(jax.random.normal(key_off, (PAIRS, PAIRS), jnp.float32), -5.0, 5.0)
    diagonal = jax.random.uniform(key_diag, (PAIRS,), jnp.float32, 1.0, 3.0)
    positions = jnp.arange(PAIRS)
    on_diag = positions[:, None] == positions[None, :]
    matrix = spread / jnp.sqrt(jnp.float32(PAIRS)) + jnp.where(on_diag, diagonal[:, None], 0.0)
    return matrix.astype(jnp.bfloat16)


def block_scale(key, shape, pieces, low, top_value):
    level = 1.0
    for axis_at, blocks in pieces:
        heights = jax.random.uniform(jax.random.fold_in(jax.random.fold_in(key, 6), axis_at), (blocks,), jnp.float32, low / len(pieces), top_value / len(pieces))
        level = level * jnp.repeat(jnp.exp(heights), shape[axis_at] // blocks).reshape((-1,) + (1,) * (len(shape) - 1 - axis_at))
    return level


def bell_draw(own_key, shape, deviation, most, cuts=(), held_as=jnp.bfloat16):
    array = deviation * jax.random.normal(own_key, shape, jnp.float32)
    if cuts:
        array = array * block_scale(own_key, shape, cuts, -0.22, 0.18)
    return jnp.clip(array, -most, most).astype(held_as)


def setup_inputs(seed: int = 0) -> dict:
    key_of = jax.random.split(jax.random.key(seed), 7)
    return {
        "amplitudes_right": draw_amplitudes_right(jax.random.fold_in(key_of[6], 71), 0),
        "amplitudes_left": draw_amplitudes_left(jax.random.fold_in(key_of[6], 71), 0),
        "previous_right": bell_draw(key_of[2], (COLS, PAIRS), 1.0, 6.0, ((1, 256),), jnp.float32),
        "previous_left": bell_draw(key_of[3], (COLS, PAIRS), 1.0, 6.0, ((1, 256),), jnp.float32),
        "coupling": jnp.clip(jax.random.uniform(key_of[4], (2, COLS), jnp.float32, 0.2, 1.0), 0.2, 1.0),
        "ladder": draw_ladder(jax.random.fold_in(key_of[6], 71), 0),
    }


def inner_mean(first, second):
    return lax.optimization_barrier(jnp.sum(first * second, axis=1)) / PAIRS

def reference(amplitudes_right, amplitudes_left, previous_right, previous_left, coupling, ladder):
    right_half = amplitudes_right.astype(jnp.bfloat16)
    left_half = amplitudes_left.astype(jnp.bfloat16)
    image_right = lax.dot_general(right_half, ladder, (((1,), (1,)), ((), ())), preferred_element_type=jnp.float32)
    image_left = jnp.dot(left_half, ladder, preferred_element_type=jnp.float32)
    alpha_now = inner_mean(amplitudes_left, image_right)
    right_res = image_right - alpha_now[:, None] * amplitudes_right - coupling[1][:, None] * previous_right
    left_res = image_left - alpha_now[:, None] * amplitudes_left - coupling[0][:, None] * previous_left
    omega_val = inner_mean(left_res, right_res)
    right_norm = inner_mean(right_res, right_res)
    left_norm = inner_mean(left_res, left_res)
    safe_omega = jnp.maximum(jnp.abs(omega_val), 0.1 * jnp.sqrt(right_norm * left_norm + 1e-06))
    beta_new = jnp.sqrt(safe_omega)
    gamma_new = omega_val / beta_new
    next_right = right_res / beta_new[:, None]
    next_left = left_res * (gamma_new / safe_omega)[:, None]
    coefficients = jnp.stack([alpha_now, beta_new, gamma_new])
    return (next_right, next_left, coefficients)
```

```python
import functools

import jax
import jax.numpy as jnp
from jax import lax
from jax.experimental import pallas as pl
from jax.experimental.pallas import tpu as pltpu
from jax.sharding import PartitionSpec as P

AXES = ("row", "col")
HALF = 64
LANES = 128
SLOTS = 16
CANCEL = 1e-3
VMEM = pl.BlockSpec(memory_space=pltpu.VMEM)
PARAMS = pltpu.CompilerParams(vmem_limit_bytes=32 * 1024 * 1024)


def lane_of(shape):
    return lax.broadcasted_iota(jnp.int32, shape, 1)


def sublane_of(shape):
    return lax.broadcasted_iota(jnp.int32, shape, 0)


def swap(tile):
    return pltpu.roll(tile, HALF, 1)


def column_of(row):
    wide = jnp.broadcast_to(row, (8, 8))
    return jnp.sum(jnp.where(lane_of((8, 8)) == sublane_of((8, 8)), wide, 0.0), axis=1, keepdims=True)


def pack_kernel(right, left, prev_right, prev_left, coupling, chunks, both, damped):
    tile = jnp.concatenate([right[...], left[...]], axis=1)
    both[...] = tile
    chunks[...] = jnp.broadcast_to(tile[None], chunks.shape)
    damped[...] = jnp.concatenate(
        [
            column_of(coupling[1:2, :]) * prev_right[...],
            column_of(coupling[0:1, :]) * prev_left[...],
        ],
        axis=1,
    )


def left_kernel(gathered, ladder, out):
    low = lane_of((8, LANES)) < HALF
    pieces = []
    for m in range(gathered.shape[0] // 2):
        pieces.append(jnp.where(low, swap(gathered[2 * m]), gathered[2 * m + 1]))
    block = jnp.concatenate(pieces, axis=1).astype(jnp.bfloat16)
    terms = jnp.dot(block, ladder[...], preferred_element_type=jnp.float32)
    for m in range(gathered.shape[0] // 2):
        piece = terms[:, LANES * m : LANES * (m + 1)]
        out[2 * m] = jnp.where(low, gathered[2 * m], swap(piece))
        out[2 * m + 1] = jnp.where(low, gathered[2 * m + 1], piece)


def right_kernel(turned, ladder, out):
    low = lane_of((8, LANES)) < HALF
    pieces = []
    for m in range(turned.shape[0] // 2):
        pieces.append(jnp.where(low, turned[2 * m], swap(turned[2 * m + 1])))
    block = jnp.concatenate(pieces, axis=1).astype(jnp.bfloat16)
    terms = lax.dot_general(
        block, ladder[...], (((1,), (1,)), ((), ())), preferred_element_type=jnp.float32
    )
    for m in range(turned.shape[0] // 2):
        piece = terms[:, LANES * m : LANES * (m + 1)]
        out[2 * m] = jnp.where(low, piece, turned[2 * m])
        out[2 * m + 1] = jnp.where(low, swap(piece), turned[2 * m + 1])


def products_kernel(partials, both, damped, rows, reduced):
    shape = (8, LANES)
    lane = lane_of(shape)
    low = lane < HALF
    image = jnp.sum(partials[...], axis=0)
    pair = both[...]
    crossed = swap(pair)
    work = image - damped[...]
    reduced[...] = work

    def total(tile):
        return jnp.sum(tile, axis=1, keepdims=True)

    def lower(tile):
        return total(jnp.where(low, tile, 0.0))

    def upper(tile):
        return total(jnp.where(low, 0.0, tile))

    own = work * pair
    square = work * work
    base = pair * pair
    dots = (
        lower(image * crossed),
        lower(work * swap(work)),
        total(work * crossed),
        lower(pair * crossed),
        lower(square),
        lower(own),
        lower(base),
        upper(square),
        upper(own),
        upper(base),
    )
    slot = lane % SLOTS
    table = jnp.zeros(shape, jnp.float32)
    for at, dot in enumerate(dots):
        table = jnp.where(slot == at, dot, table)
    row = jnp.sum(jnp.where(lane // SLOTS == sublane_of(shape), table, 0.0), axis=0, keepdims=True)
    rows[...] = jnp.broadcast_to(row, rows.shape)


def finish_kernel(pairs_total, rows, reduced, both, next_right, next_left, coefficients, flag):
    shape = (8, LANES)
    lane = lane_of(shape)
    row = jnp.sum(rows[...], axis=0, keepdims=True) / pairs_total
    table = jnp.where(lane // SLOTS == sublane_of(shape), jnp.broadcast_to(row, shape), 0.0)
    dots = [
        jnp.sum(jnp.where(lane % SLOTS == at, table, 0.0), axis=1, keepdims=True)
        for at in range(10)
    ]
    alpha = dots[0]
    omega = dots[1] - alpha * dots[2] + alpha * alpha * dots[3]
    right_norm = dots[4] - 2.0 * alpha * dots[5] + alpha * alpha * dots[6]
    left_norm = dots[7] - 2.0 * alpha * dots[8] + alpha * alpha * dots[9]
    right_safe = right_norm - CANCEL * (dots[4] + alpha * alpha * dots[6])
    left_safe = left_norm - CANCEL * (dots[7] + alpha * alpha * dots[9])
    weak = jnp.where(jnp.minimum(right_safe, left_safe) > 0.0, 0.0, 1.0)
    flag[0, 0] = jnp.max(weak).astype(jnp.int32)
    safe = jnp.maximum(
        jnp.abs(omega),
        0.1 * jnp.sqrt(jnp.maximum(right_norm, 0.0) * jnp.maximum(left_norm, 0.0) + 1e-6),
    )
    beta = jnp.sqrt(safe)
    gamma = omega / beta
    residual = reduced[...] - alpha * both[...]
    scaled = residual * jnp.where(lane < HALF, 1.0 / beta, gamma / safe)
    next_right[...] = scaled[:, :HALF]
    next_left[...] = scaled[:, HALF:]
    diagonal = lane == sublane_of(shape)
    for at, value in enumerate((alpha, beta, gamma)):
        line = jnp.sum(jnp.where(diagonal, value, 0.0), axis=0, keepdims=True)
        coefficients[at : at + 1, :] = line[:, :8]


def direct(pairs_total, reduced, both, coefficients):
    alpha = coefficients[0]
    residual = reduced - alpha[:, None] * both
    right_res, left_res = residual[:, :HALF], residual[:, HALF:]
    sums = jnp.stack(
        [
            jnp.sum(left_res * right_res, axis=1),
            jnp.sum(right_res * right_res, axis=1),
            jnp.sum(left_res * left_res, axis=1),
        ]
    )
    omega, right_norm, left_norm = lax.psum(sums, AXES) / pairs_total
    safe = jnp.maximum(jnp.abs(omega), 0.1 * jnp.sqrt(right_norm * left_norm + 1e-6))
    beta = jnp.sqrt(safe)
    gamma = omega / beta
    next_right = right_res / beta[:, None]
    next_left = left_res * (gamma / safe)[:, None]
    return next_right, next_left, jnp.stack([alpha, beta, gamma])


def local(amplitudes_right, amplitudes_left, previous_right, previous_left, coupling, ladder):
    count = lax.axis_size("col")
    devices = lax.axis_size("row") * count
    pairs_total = amplitudes_right.shape[1] * devices
    wide = jax.ShapeDtypeStruct((count, 8, LANES), jnp.float32)
    tile = jax.ShapeDtypeStruct((8, LANES), jnp.float32)
    ladder = pltpu.with_memory_space_constraint(ladder, pltpu.VMEM)

    with jax.named_scope("pack"):
        chunks, both, damped = pl.pallas_call(
            pack_kernel, out_shape=(wide, tile, tile), in_specs=[VMEM] * 5,
            out_specs=(VMEM,) * 3, compiler_params=PARAMS,
        )(amplitudes_right, amplitudes_left, previous_right, previous_left, coupling)
    gathered = lax.all_to_all(chunks, "col", 0, 0, tiled=True)
    with jax.named_scope("left_product"):
        packed = pl.pallas_call(
            left_kernel, out_shape=wide, in_specs=[VMEM] * 2, out_specs=VMEM,
            compiler_params=PARAMS,
        )(gathered, ladder)
    transpose = [(i * count + j, j * count + i) for i in range(count) for j in range(count)]
    turned = lax.ppermute(packed, AXES, transpose)
    with jax.named_scope("right_product"):
        partials = pl.pallas_call(
            right_kernel, out_shape=wide, in_specs=[VMEM] * 2, out_specs=VMEM,
            compiler_params=PARAMS,
        )(turned, ladder)
    partials = lax.all_to_all(partials, "col", 0, 0, tiled=True)
    with jax.named_scope("inner_products"):
        rows, reduced = pl.pallas_call(
            products_kernel,
            out_shape=(jax.ShapeDtypeStruct((devices, LANES), jnp.float32), tile),
            in_specs=[VMEM] * 3, out_specs=(VMEM,) * 2, compiler_params=PARAMS,
        )(partials, both, damped)
    rows = lax.all_to_all(rows, AXES, 0, 0, tiled=True)
    half = jax.ShapeDtypeStruct((8, HALF), jnp.float32)
    with jax.named_scope("finish"):
        next_right, next_left, coefficients, flag = pl.pallas_call(
            functools.partial(finish_kernel, float(pairs_total)),
            out_shape=(
                half, half, jax.ShapeDtypeStruct((3, 8), jnp.float32),
                jax.ShapeDtypeStruct((1, 1), jnp.int32),
            ),
            in_specs=[VMEM] * 3,
            out_specs=(VMEM,) * 3 + (pl.BlockSpec(memory_space=pltpu.SMEM),),
            compiler_params=PARAMS,
        )(rows, reduced, both)
    return lax.cond(
        flag[0, 0] > 0,
        lambda: direct(float(pairs_total), reduced, both, coefficients),
        lambda: (next_right, next_left, coefficients),
    )


def solution(mesh):
    placed = (
        P(None, AXES),
        P(None, AXES),
        P(None, AXES),
        P(None, AXES),
        P(),
        P("row", "col"),
    )
    return jax.shard_map(
        local,
        mesh=mesh,
        in_specs=placed,
        out_specs=(P(None, AXES), P(None, AXES), P()),
        check_vma=False,
    )
```

```python
import functools

import jax
import jax.numpy as jnp
from jax import lax
from jax.experimental import pallas as pl
from jax.experimental.pallas import tpu as pltpu
from jax.sharding import PartitionSpec as P

AXES = ("row", "col")
HALF = 64
LANES = 128
CANCEL = 1e-3
VMEM = pl.BlockSpec(memory_space=pltpu.VMEM)
HBM = pl.BlockSpec(memory_space=pltpu.HBM)
PARAMS = pltpu.CompilerParams(vmem_limit_bytes=32 * 1024 * 1024)


def lane_of(shape):
    return lax.broadcasted_iota(jnp.int32, shape, 1)


def sublane_of(shape):
    return lax.broadcasted_iota(jnp.int32, shape, 0)


def swap(tile):
    return pltpu.roll(tile, HALF, 1)


def column_of(row):
    wide = jnp.broadcast_to(row, (8, 8))
    return jnp.sum(jnp.where(lane_of((8, 8)) == sublane_of((8, 8)), wide, 0.0), axis=1, keepdims=True)


def fetch(sources, targets, sems):
    copies = [
        pltpu.make_async_copy(source, target, sems.at[at])
        for at, (source, target) in enumerate(zip(sources, targets, strict=True))
    ]
    for copy in copies:
        copy.start()
    return copies


def pack_kernel(right, left, chunks, both, right_here, left_here, sems):
    for copy in fetch((right, left), (right_here, left_here), sems):
        copy.wait()
    tile = jnp.concatenate([right_here[...], left_here[...]], axis=1)
    both[...] = tile
    chunks[...] = jnp.broadcast_to(tile[None], chunks.shape)


def left_kernel(gathered, ladder, prev_right, prev_left, coupling, out, damped):
    low = lane_of((8, LANES)) < HALF
    pieces = []
    for m in range(gathered.shape[0] // 2):
        pieces.append(jnp.where(low, swap(gathered[2 * m]), gathered[2 * m + 1]))
    block = jnp.concatenate(pieces, axis=1).astype(jnp.bfloat16)
    terms = jnp.dot(block, ladder[...], preferred_element_type=jnp.float32)
    for m in range(gathered.shape[0] // 2):
        piece = terms[:, LANES * m : LANES * (m + 1)]
        out[2 * m] = jnp.where(low, gathered[2 * m], swap(piece))
        out[2 * m + 1] = jnp.where(low, gathered[2 * m + 1], piece)
    damped[...] = jnp.concatenate(
        [
            column_of(coupling[1:2, :]) * prev_right[...],
            column_of(coupling[0:1, :]) * prev_left[...],
        ],
        axis=1,
    )


def right_kernel(turned, ladder, out):
    low = lane_of((8, LANES)) < HALF
    pieces = []
    for m in range(turned.shape[0] // 2):
        pieces.append(jnp.where(low, turned[2 * m], swap(turned[2 * m + 1])))
    block = jnp.concatenate(pieces, axis=1).astype(jnp.bfloat16)
    terms = lax.dot_general(
        block, ladder[...], (((1,), (1,)), ((), ())), preferred_element_type=jnp.float32
    )
    for m in range(turned.shape[0] // 2):
        piece = terms[:, LANES * m : LANES * (m + 1)]
        out[2 * m] = jnp.where(low, piece, turned[2 * m])
        out[2 * m + 1] = jnp.where(low, swap(piece), turned[2 * m + 1])


def products_kernel(partials, both, damped, rows, reduced):
    shape = (8, LANES)
    lane = lane_of(shape)
    low = lane < HALF
    image = jnp.sum(partials[...], axis=0)
    pair = both[...]
    crossed = swap(pair)
    work = image - damped[...]
    reduced[...] = work

    def total(tile):
        return jnp.sum(tile, axis=1, keepdims=True)

    def lower(tile):
        return total(jnp.where(low, tile, 0.0))

    def upper(tile):
        return total(jnp.where(low, 0.0, tile))

    own = work * pair
    square = work * work
    base = pair * pair
    dots = (
        lower(image * crossed),
        lower(work * swap(work)),
        total(work * crossed),
        lower(pair * crossed),
        lower(square),
        lower(own),
        lower(base),
        upper(square),
        upper(own),
        upper(base),
    )
    slot = lane // 8
    table = jnp.zeros(shape, jnp.float32)
    for at, dot in enumerate(dots):
        table = jnp.where(slot == at, dot, table)
    row = jnp.sum(jnp.where(lane % 8 == sublane_of(shape), table, 0.0), axis=0, keepdims=True)
    rows[...] = jnp.broadcast_to(row, rows.shape)


def finish_kernel(
    pairs_total, rows, reduced, both,
    next_right, next_left, coefficients, flag, right_here, left_here, coefficients_here, sems,
):
    shape = (8, LANES)
    lane = lane_of(shape)
    row = jnp.sum(rows[...], axis=0, keepdims=True) * (1.0 / pairs_total)
    wide = jnp.broadcast_to(row, shape)
    dots = [wide] + [pltpu.roll(wide, LANES - 8 * at, 1) for at in range(1, 10)]
    alpha = dots[0]
    square = alpha * alpha
    omega = dots[1] - alpha * dots[2] + square * dots[3]
    right_norm = dots[4] - 2.0 * alpha * dots[5] + square * dots[6]
    left_norm = dots[7] - 2.0 * alpha * dots[8] + square * dots[9]
    right_safe = right_norm - CANCEL * (dots[4] + square * dots[6])
    left_safe = left_norm - CANCEL * (dots[7] + square * dots[9])
    strong = jnp.minimum(right_safe, left_safe) > 0.0
    weak = jnp.where(jnp.logical_or(strong, lane >= 8), 0.0, 1.0)
    flag[0, 0] = jnp.max(weak).astype(jnp.int32)
    safe = jnp.maximum(
        jnp.abs(omega),
        0.1 * jnp.sqrt(jnp.maximum(right_norm, 0.0) * jnp.maximum(left_norm, 0.0) + 1e-6),
    )
    beta = jnp.sqrt(safe)
    gamma = omega / beta
    diagonal = lane == sublane_of(shape)

    def column(value):
        return jnp.sum(jnp.where(diagonal, value, 0.0), axis=1, keepdims=True)

    residual = reduced[...] - column(alpha) * both[...]
    scaled = residual * jnp.where(lane < HALF, column(1.0 / beta), column(gamma / safe))
    right_here[...] = scaled[:, :HALF]
    left_here[...] = scaled[:, HALF:]
    for at, value in enumerate((alpha, beta, gamma)):
        coefficients_here[at : at + 1, :] = value[:1, :8]
    targets = (next_right, next_left, coefficients)
    for copy in fetch((right_here, left_here, coefficients_here), targets, sems):
        copy.wait()


def direct(pairs_total, reduced, both, coefficients):
    alpha = coefficients[0]
    residual = reduced - alpha[:, None] * both
    right_res, left_res = residual[:, :HALF], residual[:, HALF:]
    sums = jnp.stack(
        [
            jnp.sum(left_res * right_res, axis=1),
            jnp.sum(right_res * right_res, axis=1),
            jnp.sum(left_res * left_res, axis=1),
        ]
    )
    omega, right_norm, left_norm = lax.psum(sums, AXES) / pairs_total
    safe = jnp.maximum(jnp.abs(omega), 0.1 * jnp.sqrt(right_norm * left_norm + 1e-6))
    beta = jnp.sqrt(safe)
    gamma = omega / beta
    next_right = right_res / beta[:, None]
    next_left = left_res * (gamma / safe)[:, None]
    return next_right, next_left, jnp.stack([alpha, beta, gamma])


def local(amplitudes_right, amplitudes_left, previous_right, previous_left, coupling, ladder):
    count = lax.axis_size("col")
    devices = lax.axis_size("row") * count
    pairs_total = amplitudes_right.shape[1] * devices
    wide = jax.ShapeDtypeStruct((count, 8, LANES), jnp.float32)
    tile = jax.ShapeDtypeStruct((8, LANES), jnp.float32)
    ladder = pltpu.with_memory_space_constraint(ladder, pltpu.VMEM)

    half = pltpu.VMEM((8, HALF), jnp.float32)
    stay = functools.partial(pltpu.with_memory_space_constraint, memory_space=pltpu.HBM)
    with jax.named_scope("pack"):
        chunks, both = pl.pallas_call(
            pack_kernel, out_shape=(wide, tile), in_specs=[HBM] * 2, out_specs=(VMEM,) * 2,
            scratch_shapes=[half, half, pltpu.SemaphoreType.DMA((2,))],
            cost_estimate=pl.CostEstimate(flops=10_000_000_000, bytes_accessed=65_536, transcendentals=0),
            compiler_params=PARAMS,
        )(stay(amplitudes_right), stay(amplitudes_left))
    gathered = lax.all_to_all(chunks, "col", 0, 0, tiled=True)
    with jax.named_scope("left_product"):
        packed, damped = pl.pallas_call(
            left_kernel, out_shape=(wide, tile), in_specs=[VMEM] * 5,
            out_specs=(VMEM,) * 2,
            compiler_params=PARAMS,
        )(gathered, ladder, previous_right, previous_left, coupling)
    transpose = [(i * count + j, j * count + i) for i in range(count) for j in range(count)]
    turned = lax.ppermute(packed, AXES, transpose)
    with jax.named_scope("right_product"):
        partials = pl.pallas_call(
            right_kernel, out_shape=wide, in_specs=[VMEM] * 2, out_specs=VMEM,
            compiler_params=PARAMS,
        )(turned, ladder)
    partials = lax.all_to_all(partials, "col", 0, 0, tiled=True)
    with jax.named_scope("inner_products"):
        rows, reduced = pl.pallas_call(
            products_kernel,
            out_shape=(jax.ShapeDtypeStruct((devices, LANES), jnp.float32), tile),
            in_specs=[VMEM] * 3, out_specs=(VMEM,) * 2, compiler_params=PARAMS,
        )(partials, both, damped)
    rows = lax.all_to_all(rows, AXES, 0, 0, tiled=True)
    half_out = pltpu.HBM((8, HALF), jnp.float32)
    with jax.named_scope("finish"):
        next_right, next_left, coefficients, flag = pl.pallas_call(
            functools.partial(finish_kernel, float(pairs_total)),
            out_shape=(
                half_out, half_out, pltpu.HBM((3, 8), jnp.float32),
                pltpu.SMEM((1, 1), jnp.int32),
            ),
            in_specs=[VMEM] * 3,
            out_specs=(HBM,) * 3 + (pl.BlockSpec(memory_space=pltpu.SMEM),),
            scratch_shapes=[
                half, half, pltpu.VMEM((3, 8), jnp.float32), pltpu.SemaphoreType.DMA((3,)),
            ],
            compiler_params=PARAMS,
        )(rows, reduced, both)
    return lax.cond(
        flag[0, 0] > 0,
        lambda: direct(float(pairs_total), reduced, both, coefficients),
        lambda: (next_right, next_left, coefficients),
    )


def solution(mesh):
    placed = (
        P(None, AXES),
        P(None, AXES),
        P(None, AXES),
        P(None, AXES),
        P(),
        P("row", "col"),
    )
    return jax.shard_map(
        local,
        mesh=mesh,
        in_specs=placed,
        out_specs=(P(None, AXES), P(None, AXES), P()),
        check_vma=False,
    )
```

```python
import functools

import jax
import jax.numpy as jnp
from jax import lax
from jax.experimental import pallas as pl
from jax.experimental.pallas import tpu as pltpu
from jax.sharding import PartitionSpec as P

AXES = ("row", "col")
HALF = 64
LANES = 128
CANCEL = 1e-3
VMEM = pl.BlockSpec(memory_space=pltpu.VMEM)
HBM = pl.BlockSpec(memory_space=pltpu.HBM)
PARAMS = pltpu.CompilerParams(vmem_limit_bytes=32 * 1024 * 1024)


def lane_of(shape):
    return lax.broadcasted_iota(jnp.int32, shape, 1)


def sublane_of(shape):
    return lax.broadcasted_iota(jnp.int32, shape, 0)


def swap(tile):
    return pltpu.roll(tile, HALF, 1)


def column_of(row):
    wide = jnp.broadcast_to(row, (8, 8))
    return jnp.sum(jnp.where(lane_of((8, 8)) == sublane_of((8, 8)), wide, 0.0), axis=1, keepdims=True)


def fetch(sources, targets, sems):
    copies = [
        pltpu.make_async_copy(source, target, sems.at[at])
        for at, (source, target) in enumerate(zip(sources, targets, strict=True))
    ]
    for copy in copies:
        copy.start()
    return copies


def pack_kernel(right, left, chunks, both, right_here, left_here, sems):
    for copy in fetch((right, left), (right_here, left_here), sems):
        copy.wait()
    tile = jnp.concatenate([right_here[...], left_here[...]], axis=1)
    both[...] = tile
    chunks[...] = jnp.broadcast_to(tile.astype(jnp.bfloat16)[None], chunks.shape)


def left_kernel(gathered, ladder, prev_right, prev_left, coupling, out, damped):
    low = lane_of((8, LANES)) < HALF
    rights, lefts = [], []
    for m in range(gathered.shape[0] // 2):
        even, odd = gathered[2 * m].astype(jnp.float32), gathered[2 * m + 1].astype(jnp.float32)
        rights.append(jnp.where(low, even, swap(odd)))
        lefts.append(jnp.where(low, swap(even), odd))
    block = jnp.concatenate(lefts, axis=1).astype(jnp.bfloat16)
    terms = jnp.dot(block, ladder[...], preferred_element_type=jnp.float32)
    high = terms.astype(jnp.bfloat16).astype(jnp.float32)
    rest = terms - high
    width = terms.shape[1]
    upper = jnp.concatenate(rights + [rest[:, : width // 2]], axis=1)
    lower = jnp.concatenate([high, rest[:, width // 2 :]], axis=1)
    out[...] = jnp.concatenate([upper, lower], axis=0).astype(jnp.bfloat16)
    damped[...] = jnp.concatenate(
        [
            column_of(coupling[1:2, :]) * prev_right[...],
            column_of(coupling[0:1, :]) * prev_left[...],
        ],
        axis=1,
    )


def right_kernel(turned, ladder, out):
    low = lane_of((8, LANES)) < HALF
    width = ladder.shape[1]
    block = turned[:, :width][:8]
    terms = lax.dot_general(
        block, ladder[...], (((1,), (1,)), ((), ())), preferred_element_type=jnp.float32
    )
    for m in range(out.shape[0] // 2):
        at = LANES * m
        side = at % (width // 2)
        half = 8 * (at // (width // 2))
        high = turned[:, at : at + LANES].astype(jnp.float32)[8:]
        rest = turned[:, width + side : width + side + LANES].astype(jnp.float32)[half : half + 8]
        left = high + rest
        piece = terms[:, at : at + LANES]
        out[2 * m] = jnp.where(low, piece, swap(left))
        out[2 * m + 1] = jnp.where(low, swap(piece), left)


def products_kernel(partials, both, damped, rows, reduced):
    shape = (8, LANES)
    lane = lane_of(shape)
    low = lane < HALF
    image = jnp.sum(partials[...], axis=0)
    pair = both[...]
    crossed = swap(pair)
    work = image - damped[...]
    reduced[...] = work

    def total(tile):
        return jnp.sum(tile, axis=1, keepdims=True)

    def lower(tile):
        return total(jnp.where(low, tile, 0.0))

    def upper(tile):
        return total(jnp.where(low, 0.0, tile))

    own = work * pair
    square = work * work
    base = pair * pair
    dots = (
        lower(image * crossed),
        lower(work * swap(work)),
        total(work * crossed),
        lower(pair * crossed),
        lower(square),
        lower(own),
        lower(base),
        upper(square),
        upper(own),
        upper(base),
    )
    slot = lane // 8
    table = jnp.zeros(shape, jnp.float32)
    for at, dot in enumerate(dots):
        table = jnp.where(slot == at, dot, table)
    row = jnp.sum(jnp.where(lane % 8 == sublane_of(shape), table, 0.0), axis=0, keepdims=True)
    rows[...] = jnp.broadcast_to(row, rows.shape)


def finish_kernel(
    pairs_total, rows, reduced, both,
    next_right, next_left, coefficients, flag, right_here, left_here, coefficients_here, sems,
):
    shape = (8, LANES)
    lane = lane_of(shape)
    row = jnp.sum(rows[...], axis=0, keepdims=True) * (1.0 / pairs_total)
    wide = jnp.broadcast_to(row, shape)
    dots = [wide] + [pltpu.roll(wide, LANES - 8 * at, 1) for at in range(1, 10)]
    alpha = dots[0]
    square = alpha * alpha
    omega = dots[1] - alpha * dots[2] + square * dots[3]
    right_norm = dots[4] - 2.0 * alpha * dots[5] + square * dots[6]
    left_norm = dots[7] - 2.0 * alpha * dots[8] + square * dots[9]
    safe = jnp.maximum(
        jnp.abs(omega),
        0.1 * jnp.sqrt(jnp.maximum(right_norm, 0.0) * jnp.maximum(left_norm, 0.0) + 1e-6),
    )
    beta = jnp.sqrt(safe)
    gamma = omega / beta
    diagonal = lane == sublane_of(shape)

    def column(value):
        return jnp.sum(jnp.where(diagonal, value, 0.0), axis=1, keepdims=True)

    residual = reduced[...] - column(alpha) * both[...]
    scaled = residual * jnp.where(lane < HALF, column(1.0 / beta), column(gamma / safe))
    right_here[...] = scaled[:, :HALF]
    left_here[...] = scaled[:, HALF:]
    for at, value in enumerate((alpha, beta, gamma)):
        coefficients_here[at : at + 1, :] = value[:1, :8]
    targets = (next_right, next_left, coefficients)
    copies = fetch((right_here, left_here, coefficients_here), targets, sems)
    right_safe = right_norm - CANCEL * (dots[4] + square * dots[6])
    left_safe = left_norm - CANCEL * (dots[7] + square * dots[9])
    strong = jnp.minimum(right_safe, left_safe) > 0.0
    weak = jnp.where(jnp.logical_or(strong, lane >= 8), 0.0, 1.0)
    flag[0, 0] = jnp.max(weak).astype(jnp.int32)
    for copy in copies:
        copy.wait()


def direct(pairs_total, reduced, both, coefficients):
    alpha = coefficients[0]
    residual = reduced - alpha[:, None] * both
    right_res, left_res = residual[:, :HALF], residual[:, HALF:]
    sums = jnp.stack(
        [
            jnp.sum(left_res * right_res, axis=1),
            jnp.sum(right_res * right_res, axis=1),
            jnp.sum(left_res * left_res, axis=1),
        ]
    )
    omega, right_norm, left_norm = lax.psum(sums, AXES) / pairs_total
    safe = jnp.maximum(jnp.abs(omega), 0.1 * jnp.sqrt(right_norm * left_norm + 1e-6))
    beta = jnp.sqrt(safe)
    gamma = omega / beta
    next_right = right_res / beta[:, None]
    next_left = left_res * (gamma / safe)[:, None]
    return next_right, next_left, jnp.stack([alpha, beta, gamma])


def local(amplitudes_right, amplitudes_left, previous_right, previous_left, coupling, ladder):
    count = lax.axis_size("col")
    devices = lax.axis_size("row") * count
    pairs_total = amplitudes_right.shape[1] * devices
    wide = jax.ShapeDtypeStruct((count, 8, LANES), jnp.float32)
    thin = jax.ShapeDtypeStruct((count, 8, LANES), jnp.bfloat16)
    block = ladder.shape[1]
    folded = jax.ShapeDtypeStruct((16, block + block // 2), jnp.bfloat16)
    tile = jax.ShapeDtypeStruct((8, LANES), jnp.float32)
    ladder = pltpu.with_memory_space_constraint(ladder, pltpu.VMEM)

    half = pltpu.VMEM((8, HALF), jnp.float32)
    stay = functools.partial(pltpu.with_memory_space_constraint, memory_space=pltpu.HBM)
    with jax.named_scope("pack"):
        chunks, both = pl.pallas_call(
            pack_kernel, out_shape=(thin, tile), in_specs=[HBM] * 2, out_specs=(VMEM,) * 2,
            scratch_shapes=[half, half, pltpu.SemaphoreType.DMA((2,))],
            cost_estimate=pl.CostEstimate(flops=10_000_000_000, bytes_accessed=65_536, transcendentals=0),
            compiler_params=PARAMS,
        )(stay(amplitudes_right), stay(amplitudes_left))
    gathered = lax.all_to_all(chunks, "col", 0, 0, tiled=True)
    with jax.named_scope("left_product"):
        packed, damped = pl.pallas_call(
            left_kernel, out_shape=(folded, tile), in_specs=[VMEM] * 5,
            out_specs=(VMEM,) * 2,
            compiler_params=PARAMS,
        )(gathered, ladder, previous_right, previous_left, coupling)
    transpose = [(i * count + j, j * count + i) for i in range(count) for j in range(count)]
    turned = lax.ppermute(packed, AXES, transpose)
    with jax.named_scope("right_product"):
        partials = pl.pallas_call(
            right_kernel, out_shape=wide, in_specs=[VMEM] * 2, out_specs=VMEM,
            compiler_params=PARAMS,
        )(turned, ladder)
    partials = lax.all_to_all(partials, "col", 0, 0, tiled=True)
    with jax.named_scope("inner_products"):
        rows, reduced = pl.pallas_call(
            products_kernel,
            out_shape=(jax.ShapeDtypeStruct((devices, LANES), jnp.float32), tile),
            in_specs=[VMEM] * 3, out_specs=(VMEM,) * 2, compiler_params=PARAMS,
        )(partials, both, damped)
    rows = lax.all_to_all(rows, AXES, 0, 0, tiled=True)
    half_out = pltpu.HBM((8, HALF), jnp.float32)
    with jax.named_scope("finish"):
        next_right, next_left, coefficients, flag = pl.pallas_call(
            functools.partial(finish_kernel, float(pairs_total)),
            out_shape=(
                half_out, half_out, pltpu.HBM((3, 8), jnp.float32),
                pltpu.SMEM((1, 1), jnp.int32),
            ),
            in_specs=[VMEM] * 3,
            out_specs=(HBM,) * 3 + (pl.BlockSpec(memory_space=pltpu.SMEM),),
            scratch_shapes=[
                half, half, pltpu.VMEM((3, 8), jnp.float32), pltpu.SemaphoreType.DMA((3,)),
            ],
            compiler_params=PARAMS,
        )(rows, reduced, both)
    return lax.cond(
        flag[0, 0] > 0,
        lambda: direct(float(pairs_total), reduced, both, coefficients),
        lambda: (next_right, next_left, coefficients),
    )


def solution(mesh):
    placed = (
        P(None, AXES),
        P(None, AXES),
        P(None, AXES),
        P(None, AXES),
        P(),
        P("row", "col"),
    )
    return jax.shard_map(
        local,
        mesh=mesh,
        in_specs=placed,
        out_specs=(P(None, AXES), P(None, AXES), P()),
        check_vma=False,
    )
```

```python
import functools

import jax
import jax.numpy as jnp
from jax import lax
from jax.experimental import pallas as pl
from jax.experimental.pallas import tpu as pltpu
from jax.sharding import PartitionSpec as P

ROW = ("row",)
COL = ("chip", "core")
AXES = ROW + COL
HALF = 64
LANES = 128
CANCEL = 1e-3
VMEM = pl.BlockSpec(memory_space=pltpu.VMEM)
HBM = pl.BlockSpec(memory_space=pltpu.HBM)
PARAMS = pltpu.CompilerParams(vmem_limit_bytes=32 * 1024 * 1024)


def lane_of(shape):
    return lax.broadcasted_iota(jnp.int32, shape, 1)


def sublane_of(shape):
    return lax.broadcasted_iota(jnp.int32, shape, 0)


def swap(tile):
    return pltpu.roll(tile, HALF, 1)


def column_of(row):
    wide = jnp.broadcast_to(row, (8, 8))
    return jnp.sum(jnp.where(lane_of((8, 8)) == sublane_of((8, 8)), wide, 0.0), axis=1, keepdims=True)


def fetch(sources, targets, sems):
    copies = [
        pltpu.make_async_copy(source, target, sems.at[at])
        for at, (source, target) in enumerate(zip(sources, targets, strict=True))
    ]
    for copy in copies:
        copy.start()
    return copies


def pack_kernel(right, left, chunks, both, right_here, left_here, sems):
    for copy in fetch((right, left), (right_here, left_here), sems):
        copy.wait()
    tile = jnp.concatenate([right_here[...], left_here[...]], axis=1)
    both[...] = tile
    chunks[...] = jnp.broadcast_to(tile.astype(jnp.bfloat16)[None], chunks.shape)


def left_kernel(gathered, ladder, prev_right, prev_left, coupling, out, damped):
    low = lane_of((8, LANES)) < HALF
    rights, lefts = [], []
    for m in range(gathered.shape[0] // 2):
        even, odd = gathered[2 * m].astype(jnp.float32), gathered[2 * m + 1].astype(jnp.float32)
        rights.append(jnp.where(low, even, swap(odd)))
        lefts.append(jnp.where(low, swap(even), odd))
    block = jnp.concatenate(lefts, axis=1).astype(jnp.bfloat16)
    terms = jnp.dot(block, ladder[...], preferred_element_type=jnp.float32)
    high = terms.astype(jnp.bfloat16).astype(jnp.float32)
    rest = terms - high
    width = terms.shape[1]
    upper = jnp.concatenate(rights + [rest[:, : width // 2]], axis=1)
    lower = jnp.concatenate([high, rest[:, width // 2 :]], axis=1)
    out[...] = jnp.concatenate([upper, lower], axis=0).astype(jnp.bfloat16)
    damped[...] = jnp.concatenate(
        [
            column_of(coupling[1:2, :]) * prev_right[...],
            column_of(coupling[0:1, :]) * prev_left[...],
        ],
        axis=1,
    )


def right_kernel(turned, ladder, out):
    low = lane_of((8, LANES)) < HALF
    width = ladder.shape[1]
    block = turned[:, :width][:8]
    terms = lax.dot_general(
        block, ladder[...], (((1,), (1,)), ((), ())), preferred_element_type=jnp.float32
    )
    for m in range(out.shape[0] // 2):
        at = LANES * m
        side = at % (width // 2)
        half = 8 * (at // (width // 2))
        high = turned[:, at : at + LANES].astype(jnp.float32)[8:]
        rest = turned[:, width + side : width + side + LANES].astype(jnp.float32)[half : half + 8]
        left = high + rest
        piece = terms[:, at : at + LANES]
        out[2 * m] = jnp.where(low, piece, swap(left))
        out[2 * m + 1] = jnp.where(low, swap(piece), left)


def products_kernel(partials, both, damped, rows, reduced):
    shape = (8, LANES)
    lane = lane_of(shape)
    low = lane < HALF
    image = jnp.sum(partials[...], axis=0)
    pair = both[...]
    crossed = swap(pair)
    work = image - damped[...]
    reduced[...] = work

    def total(tile):
        return jnp.sum(tile, axis=1, keepdims=True)

    def lower(tile):
        return total(jnp.where(low, tile, 0.0))

    def upper(tile):
        return total(jnp.where(low, 0.0, tile))

    own = work * pair
    square = work * work
    base = pair * pair
    dots = (
        lower(image * crossed),
        lower(work * swap(work)),
        total(work * crossed),
        lower(pair * crossed),
        lower(square),
        lower(own),
        lower(base),
        upper(square),
        upper(own),
        upper(base),
    )
    slot = lane // 8
    table = jnp.zeros(shape, jnp.float32)
    for at, dot in enumerate(dots):
        table = jnp.where(slot == at, dot, table)
    row = jnp.sum(jnp.where(lane % 8 == sublane_of(shape), table, 0.0), axis=0, keepdims=True)
    rows[...] = jnp.broadcast_to(row, rows.shape)


def finish_kernel(
    pairs_total, rows, reduced, both,
    next_right, next_left, coefficients, flag, right_here, left_here, coefficients_here, sems,
):
    shape = (8, LANES)
    lane = lane_of(shape)
    row = jnp.sum(rows[...], axis=0, keepdims=True) * (1.0 / pairs_total)
    wide = jnp.broadcast_to(row, shape)
    dots = [wide] + [pltpu.roll(wide, LANES - 8 * at, 1) for at in range(1, 10)]
    alpha = dots[0]
    square = alpha * alpha
    omega = dots[1] - alpha * dots[2] + square * dots[3]
    right_norm = dots[4] - 2.0 * alpha * dots[5] + square * dots[6]
    left_norm = dots[7] - 2.0 * alpha * dots[8] + square * dots[9]
    safe = jnp.maximum(
        jnp.abs(omega),
        0.1 * jnp.sqrt(jnp.maximum(right_norm, 0.0) * jnp.maximum(left_norm, 0.0) + 1e-6),
    )
    beta = jnp.sqrt(safe)
    gamma = omega / beta
    diagonal = lane == sublane_of(shape)

    def column(value):
        return jnp.sum(jnp.where(diagonal, value, 0.0), axis=1, keepdims=True)

    residual = reduced[...] - column(alpha) * both[...]
    scaled = residual * jnp.where(lane < HALF, column(1.0 / beta), column(gamma / safe))
    right_here[...] = scaled[:, :HALF]
    left_here[...] = scaled[:, HALF:]
    for at, value in enumerate((alpha, beta, gamma)):
        coefficients_here[at : at + 1, :] = value[:1, :8]
    targets = (next_right, next_left, coefficients)
    copies = fetch((right_here, left_here, coefficients_here), targets, sems)
    right_safe = right_norm - CANCEL * (dots[4] + square * dots[6])
    left_safe = left_norm - CANCEL * (dots[7] + square * dots[9])
    strong = jnp.minimum(right_safe, left_safe) > 0.0
    weak = jnp.where(jnp.logical_or(strong, lane >= 8), 0.0, 1.0)
    flag[0, 0] = jnp.max(weak).astype(jnp.int32)
    for copy in copies:
        copy.wait()


def direct(pairs_total, reduced, both, coefficients):
    alpha = coefficients[0]
    residual = reduced - alpha[:, None] * both
    right_res, left_res = residual[:, :HALF], residual[:, HALF:]
    sums = jnp.stack(
        [
            jnp.sum(left_res * right_res, axis=1),
            jnp.sum(right_res * right_res, axis=1),
            jnp.sum(left_res * left_res, axis=1),
        ]
    )
    omega, right_norm, left_norm = lax.psum(sums, AXES) / pairs_total
    safe = jnp.maximum(jnp.abs(omega), 0.1 * jnp.sqrt(right_norm * left_norm + 1e-6))
    beta = jnp.sqrt(safe)
    gamma = omega / beta
    next_right = right_res / beta[:, None]
    next_left = left_res * (gamma / safe)[:, None]
    return next_right, next_left, jnp.stack([alpha, beta, gamma])


def local(amplitudes_right, amplitudes_left, previous_right, previous_left, coupling, ladder):
    count = lax.axis_size(COL)
    devices = lax.axis_size(ROW) * count
    pairs_total = amplitudes_right.shape[1] * devices
    wide = jax.ShapeDtypeStruct((count, 8, LANES), jnp.float32)
    thin = jax.ShapeDtypeStruct((count, 8, LANES), jnp.bfloat16)
    block = ladder.shape[1]
    folded = jax.ShapeDtypeStruct((16, block + block // 2), jnp.bfloat16)
    tile = jax.ShapeDtypeStruct((8, LANES), jnp.float32)
    ladder = pltpu.with_memory_space_constraint(ladder, pltpu.VMEM)

    half = pltpu.VMEM((8, HALF), jnp.float32)
    stay = functools.partial(pltpu.with_memory_space_constraint, memory_space=pltpu.HBM)
    with jax.named_scope("pack"):
        chunks, both = pl.pallas_call(
            pack_kernel, out_shape=(thin, tile), in_specs=[HBM] * 2, out_specs=(VMEM,) * 2,
            scratch_shapes=[half, half, pltpu.SemaphoreType.DMA((2,))],
            cost_estimate=pl.CostEstimate(flops=10_000_000_000, bytes_accessed=65_536, transcendentals=0),
            compiler_params=PARAMS,
        )(stay(amplitudes_right), stay(amplitudes_left))
    gathered = lax.all_to_all(chunks, COL, 0, 0, tiled=True)
    with jax.named_scope("left_product"):
        packed, damped = pl.pallas_call(
            left_kernel, out_shape=(folded, tile), in_specs=[VMEM] * 5,
            out_specs=(VMEM,) * 2,
            compiler_params=PARAMS,
        )(gathered, ladder, previous_right, previous_left, coupling)
    transpose = [(i * count + j, j * count + i) for i in range(count) for j in range(count)]
    turned = lax.ppermute(packed, AXES, transpose)
    with jax.named_scope("right_product"):
        partials = pl.pallas_call(
            right_kernel, out_shape=wide, in_specs=[VMEM] * 2, out_specs=VMEM,
            compiler_params=PARAMS,
        )(turned, ladder)
    partials = lax.all_to_all(partials, COL, 0, 0, tiled=True)
    with jax.named_scope("inner_products"):
        rows, reduced = pl.pallas_call(
            products_kernel,
            out_shape=(tile, tile),
            in_specs=[VMEM] * 3, out_specs=(VMEM,) * 2, compiler_params=PARAMS,
        )(partials, both, damped)
    other = lax.ppermute(rows, "core", ((0, 1), (1, 0)))
    with jax.named_scope("chip_total"):
        rows = jnp.broadcast_to((rows + other)[:1], (devices // 2, LANES))
    rows = lax.all_to_all(rows, ROW + COL[:1], 0, 0, tiled=True)
    half_out = pltpu.HBM((8, HALF), jnp.float32)
    with jax.named_scope("finish"):
        next_right, next_left, coefficients, flag = pl.pallas_call(
            functools.partial(finish_kernel, float(pairs_total)),
            out_shape=(
                half_out, half_out, pltpu.HBM((3, 8), jnp.float32),
                pltpu.SMEM((1, 1), jnp.int32),
            ),
            in_specs=[VMEM] * 3,
            out_specs=(HBM,) * 3 + (pl.BlockSpec(memory_space=pltpu.SMEM),),
            scratch_shapes=[
                half, half, pltpu.VMEM((3, 8), jnp.float32), pltpu.SemaphoreType.DMA((3,)),
            ],
            compiler_params=PARAMS,
        )(rows, reduced, both)
    return lax.cond(
        flag[0, 0] > 0,
        lambda: direct(float(pairs_total), reduced, both, coefficients),
        lambda: (next_right, next_left, coefficients),
    )


def solution(mesh):
    rows_count, cols_count = mesh.devices.shape
    mesh = jax.sharding.Mesh(mesh.devices.reshape(rows_count, cols_count // 2, 2), ROW + COL)
    placed = (
        P(None, AXES),
        P(None, AXES),
        P(None, AXES),
        P(None, AXES),
        P(),
        P(ROW, COL),
    )
    return jax.shard_map(
        local,
        mesh=mesh,
        in_specs=placed,
        out_specs=(P(None, AXES), P(None, AXES), P()),
        check_vma=False,
    )
```

```python
import functools

import jax
import jax.numpy as jnp
from jax import lax
from jax.experimental import pallas as pl
from jax.experimental.pallas import tpu as pltpu
from jax.sharding import PartitionSpec as P

ROW = ("row",)
COL = ("far", "chip", "core")
AXES = ROW + COL
HALF = 64
LANES = 128
CANCEL = 1e-3
VMEM = pl.BlockSpec(memory_space=pltpu.VMEM)
HBM = pl.BlockSpec(memory_space=pltpu.HBM)
PARAMS = pltpu.CompilerParams(vmem_limit_bytes=32 * 1024 * 1024)


def lane_of(shape):
    return lax.broadcasted_iota(jnp.int32, shape, 1)


def sublane_of(shape):
    return lax.broadcasted_iota(jnp.int32, shape, 0)


def swap(tile):
    return pltpu.roll(tile, HALF, 1)


def column_of(row):
    wide = jnp.broadcast_to(row, (8, 8))
    return jnp.sum(jnp.where(lane_of((8, 8)) == sublane_of((8, 8)), wide, 0.0), axis=1, keepdims=True)


def fetch(sources, targets, sems):
    copies = [
        pltpu.make_async_copy(source, target, sems.at[at])
        for at, (source, target) in enumerate(zip(sources, targets, strict=True))
    ]
    for copy in copies:
        copy.start()
    return copies


def pack_kernel(
    right, left, prev_right, prev_left, coupling,
    chunks, both, right_here, left_here, prev_right_here, prev_left_here, coupling_here, sems,
):
    sources = (right, left, prev_right, prev_left, coupling)
    targets = (right_here, left_here, prev_right_here, prev_left_here, coupling_here)
    for copy in fetch(sources, targets, sems):
        copy.wait()
    tile = jnp.concatenate([right_here[...], left_here[...]], axis=1)
    damped = jnp.concatenate(
        [
            column_of(coupling_here[1:2, :]) * prev_right_here[...],
            column_of(coupling_here[0:1, :]) * prev_left_here[...],
        ],
        axis=1,
    )
    both[...] = tile
    chunks[...] = jnp.broadcast_to(jnp.concatenate([tile, damped], axis=0)[None], chunks.shape)


def left_kernel(gathered, ladder, out):
    low = lane_of((8, LANES)) < HALF
    rights, lefts = [], []
    for m in range(gathered.shape[0] // 2):
        even, odd = gathered[2 * m, :8], gathered[2 * m + 1, :8]
        rights.append(jnp.where(low, even, swap(odd)))
        lefts.append(jnp.where(low, swap(even), odd))
    block = jnp.concatenate(lefts, axis=1).astype(jnp.bfloat16)
    terms = jnp.dot(block, ladder[...], preferred_element_type=jnp.float32)
    high = terms.astype(jnp.bfloat16).astype(jnp.float32)
    rest = terms - high
    width = terms.shape[1]
    upper = jnp.concatenate(rights + [rest[:, : width // 2]], axis=1)
    lower = jnp.concatenate([high, rest[:, width // 2 :]], axis=1)
    out[...] = jnp.concatenate([upper, lower], axis=0).astype(jnp.bfloat16)


def right_kernel(turned, ladder, out):
    low = lane_of((8, LANES)) < HALF
    width = ladder.shape[1]
    block = turned[:, :width][:8]
    terms = lax.dot_general(
        block, ladder[...], (((1,), (1,)), ((), ())), preferred_element_type=jnp.float32
    )
    tiles = []
    for m in range(out.shape[0] // 2):
        at = LANES * m
        side = at % (width // 2)
        half = 8 * (at // (width // 2))
        high = turned[:, at : at + LANES].astype(jnp.float32)[8:]
        rest = turned[:, width + side : width + side + LANES].astype(jnp.float32)[half : half + 8]
        left = high + rest
        piece = terms[:, at : at + LANES]
        tiles.append(jnp.where(low, piece, swap(left)))
        tiles.append(jnp.where(low, swap(piece), left))
    half = len(tiles) // 2
    for at, tile in enumerate(tiles):
        for far in range(2):
            out[far * half + at % half, at // half] = tile


def products_kernel(partials, gathered, rows, reduced):
    shape = (8, LANES)
    lane = lane_of(shape)
    low = lane < HALF
    half = partials.shape[0] // 2
    near = lax.axis_index("chip") * lax.axis_size("core") + lax.axis_index("core")
    mine = lax.axis_index("far")
    tiles = [0.0] * 7
    for far in range(2):
        chunk = gathered[far * half + near]
        pair, damped = chunk[:8], chunk[8:]
        image = jnp.sum(partials[:, far], axis=0)
        crossed = swap(pair)
        work = image - damped

        @pl.when(mine == far)
        def _(work=work):
            reduced[...] = work

        terms = (
            image * crossed, work * swap(work), work * crossed, pair * crossed,
            work * work, work * pair, pair * pair,
        )
        tiles = [tile + term for tile, term in zip(tiles, terms, strict=True)]
    first, cross, mixed, base_cross, square, own, base = tiles

    def total(tile):
        return jnp.sum(tile, axis=1, keepdims=True)

    def lower(tile):
        return total(jnp.where(low, tile, 0.0))

    def upper(tile):
        return total(jnp.where(low, 0.0, tile))

    dots = (
        lower(first), lower(cross), total(mixed), lower(base_cross), lower(square),
        lower(own), lower(base), upper(square), upper(own), upper(base),
    )
    slot = lane // 8
    table = jnp.zeros(shape, jnp.float32)
    for at, dot in enumerate(dots):
        table = jnp.where(slot == at, dot, table)
    row = jnp.sum(jnp.where(lane % 8 == sublane_of(shape), table, 0.0), axis=0, keepdims=True)
    rows[...] = jnp.broadcast_to(row, rows.shape)


def finish_kernel(
    pairs_total, rows, reduced, both,
    next_right, next_left, coefficients, flag, right_here, left_here, coefficients_here, sems,
):
    shape = (8, LANES)
    lane = lane_of(shape)
    row = jnp.sum(rows[...], axis=0, keepdims=True) * (1.0 / pairs_total)
    wide = jnp.broadcast_to(row, shape)
    dots = [wide] + [pltpu.roll(wide, LANES - 8 * at, 1) for at in range(1, 10)]
    alpha = dots[0]
    square = alpha * alpha
    omega = dots[1] - alpha * dots[2] + square * dots[3]
    right_norm = dots[4] - 2.0 * alpha * dots[5] + square * dots[6]
    left_norm = dots[7] - 2.0 * alpha * dots[8] + square * dots[9]
    safe = jnp.maximum(
        jnp.abs(omega),
        0.1 * jnp.sqrt(jnp.maximum(right_norm, 0.0) * jnp.maximum(left_norm, 0.0) + 1e-6),
    )
    beta = jnp.sqrt(safe)
    gamma = omega / beta
    diagonal = lane == sublane_of(shape)

    def column(value):
        return jnp.sum(jnp.where(diagonal, value, 0.0), axis=1, keepdims=True)

    residual = reduced[...] - column(alpha) * both[...]
    scaled = residual * jnp.where(lane < HALF, column(1.0 / beta), column(gamma / safe))
    right_here[...] = scaled[:, :HALF]
    left_here[...] = scaled[:, HALF:]
    for at, value in enumerate((alpha, beta, gamma)):
        coefficients_here[at : at + 1, :] = value[:1, :8]
    targets = (next_right, next_left, coefficients)
    copies = fetch((right_here, left_here, coefficients_here), targets, sems)
    right_safe = right_norm - CANCEL * (dots[4] + square * dots[6])
    left_safe = left_norm - CANCEL * (dots[7] + square * dots[9])
    strong = jnp.minimum(right_safe, left_safe) > 0.0
    weak = jnp.where(jnp.logical_or(strong, lane >= 8), 0.0, 1.0)
    flag[0, 0] = jnp.max(weak).astype(jnp.int32)
    for copy in copies:
        copy.wait()


def direct(pairs_total, reduced, both, coefficients):
    alpha = coefficients[0]
    residual = reduced - alpha[:, None] * both
    right_res, left_res = residual[:, :HALF], residual[:, HALF:]
    sums = jnp.stack(
        [
            jnp.sum(left_res * right_res, axis=1),
            jnp.sum(right_res * right_res, axis=1),
            jnp.sum(left_res * left_res, axis=1),
        ]
    )
    omega, right_norm, left_norm = lax.psum(sums, AXES) / pairs_total
    safe = jnp.maximum(jnp.abs(omega), 0.1 * jnp.sqrt(right_norm * left_norm + 1e-6))
    beta = jnp.sqrt(safe)
    gamma = omega / beta
    next_right = right_res / beta[:, None]
    next_left = left_res * (gamma / safe)[:, None]
    return next_right, next_left, jnp.stack([alpha, beta, gamma])


def local(amplitudes_right, amplitudes_left, previous_right, previous_left, coupling, ladder):
    count = lax.axis_size(COL)
    devices = lax.axis_size(ROW) * count
    pairs_total = amplitudes_right.shape[1] * devices
    block = ladder.shape[1]
    folded = jax.ShapeDtypeStruct((16, block + block // 2), jnp.bfloat16)
    tile = jax.ShapeDtypeStruct((8, LANES), jnp.float32)
    ladder = pltpu.with_memory_space_constraint(ladder, pltpu.VMEM)

    half = pltpu.VMEM((8, HALF), jnp.float32)
    stay = functools.partial(pltpu.with_memory_space_constraint, memory_space=pltpu.HBM)
    with jax.named_scope("pack"):
        chunks, both = pl.pallas_call(
            pack_kernel,
            out_shape=(jax.ShapeDtypeStruct((count, 16, LANES), jnp.float32), tile),
            in_specs=[HBM] * 5, out_specs=(VMEM,) * 2,
            scratch_shapes=[half] * 4
            + [pltpu.VMEM((2, 8), jnp.float32), pltpu.SemaphoreType.DMA((5,))],
            cost_estimate=pl.CostEstimate(
                flops=10_000_000_000, bytes_accessed=65_536, transcendentals=0
            ),
            compiler_params=PARAMS,
        )(
            stay(amplitudes_right), stay(amplitudes_left), stay(previous_right),
            stay(previous_left), stay(coupling),
        )
    gathered = lax.all_to_all(chunks, COL, 0, 0, tiled=True)
    with jax.named_scope("left_product"):
        packed = pl.pallas_call(
            left_kernel, out_shape=folded, in_specs=[VMEM] * 2, out_specs=VMEM,
            compiler_params=PARAMS,
        )(gathered, ladder)
    transpose = [(i * count + j, j * count + i) for i in range(count) for j in range(count)]
    turned = lax.ppermute(packed, AXES, transpose)
    with jax.named_scope("right_product"):
        partials = pl.pallas_call(
            right_kernel, out_shape=jax.ShapeDtypeStruct((count, 2, 8, LANES), jnp.float32), in_specs=[VMEM] * 2, out_specs=VMEM,
            compiler_params=PARAMS,
        )(turned, ladder)
    partials = lax.all_to_all(partials, COL, 0, 0, tiled=True)
    with jax.named_scope("inner_products"):
        rows, reduced = pl.pallas_call(
            products_kernel,
            out_shape=(tile, tile),
            in_specs=[VMEM] * 2, out_specs=(VMEM,) * 2, compiler_params=PARAMS,
        )(partials, gathered)
    other = lax.ppermute(rows, "core", ((0, 1), (1, 0)))
    with jax.named_scope("chip_total"):
        rows = jnp.broadcast_to((rows + other)[:1], (devices // 4, LANES))
    rows = lax.all_to_all(rows, ROW + COL[1:2], 0, 0, tiled=True)
    half_out = pltpu.HBM((8, HALF), jnp.float32)
    with jax.named_scope("finish"):
        next_right, next_left, coefficients, flag = pl.pallas_call(
            functools.partial(finish_kernel, float(pairs_total)),
            out_shape=(
                half_out, half_out, pltpu.HBM((3, 8), jnp.float32),
                pltpu.SMEM((1, 1), jnp.int32),
            ),
            in_specs=[VMEM] * 3,
            out_specs=(HBM,) * 3 + (pl.BlockSpec(memory_space=pltpu.SMEM),),
            scratch_shapes=[
                half, half, pltpu.VMEM((3, 8), jnp.float32), pltpu.SemaphoreType.DMA((3,)),
            ],
            compiler_params=PARAMS,
        )(rows, reduced, both)
    return lax.cond(
        flag[0, 0] > 0,
        lambda: direct(float(pairs_total), reduced, both, coefficients),
        lambda: (next_right, next_left, coefficients),
    )


def solution(mesh):
    rows_count, cols_count = mesh.devices.shape
    mesh = jax.sharding.Mesh(mesh.devices.reshape(rows_count, 2, cols_count // 4, 2), ROW + COL)
    placed = (
        P(None, AXES),
        P(None, AXES),
        P(None, AXES),
        P(None, AXES),
        P(),
        P(ROW, COL),
    )
    return jax.shard_map(
        local,
        mesh=mesh,
        in_specs=placed,
        out_specs=(P(None, AXES), P(None, AXES), P()),
        check_vma=False,
    )
```

```python
import functools

import jax
import jax.numpy as jnp
from jax import lax
from jax.experimental import pallas as pl
from jax.experimental.pallas import tpu as pltpu
from jax.sharding import PartitionSpec as P

ROW = ("row",)
COL = ("far", "chip", "core")
AXES = ROW + COL
HALF = 64
LANES = 128
CHUNK = 17
CANCEL = 1e-3
VMEM = pl.BlockSpec(memory_space=pltpu.VMEM)
HBM = pl.BlockSpec(memory_space=pltpu.HBM)
PARAMS = pltpu.CompilerParams(vmem_limit_bytes=32 * 1024 * 1024)


def lane_of(shape):
    return lax.broadcasted_iota(jnp.int32, shape, 1)


def sublane_of(shape):
    return lax.broadcasted_iota(jnp.int32, shape, 0)


def swap(tile):
    return pltpu.roll(tile, HALF, 1)


def column_of(row):
    wide = jnp.broadcast_to(row, (8, 8))
    return jnp.sum(jnp.where(lane_of((8, 8)) == sublane_of((8, 8)), wide, 0.0), axis=1, keepdims=True)


def fetch(sources, targets, sems):
    copies = [
        pltpu.make_async_copy(source, target, sems.at[at])
        for at, (source, target) in enumerate(zip(sources, targets, strict=True))
    ]
    for copy in copies:
        copy.start()
    return copies


def pack_kernel(right, left, chunks, both, right_here, left_here, sems):
    for copy in fetch((right, left), (right_here, left_here), sems):
        copy.wait()
    tile = jnp.concatenate([right_here[...], left_here[...]], axis=1)
    both[...] = tile
    chunks[...] = jnp.broadcast_to(tile[None], chunks.shape)


def left_kernel(
    gathered, ladder, both, prev_right, prev_left, coupling, out, damped, missing
):
    low = lane_of((8, LANES)) < HALF
    rights, lefts = [], []
    for m in range(gathered.shape[0] // 2):
        even, odd = gathered[2 * m], gathered[2 * m + 1]
        rights.append(jnp.where(low, even, swap(odd)))
        lefts.append(jnp.where(low, swap(even), odd))
    block = jnp.concatenate(lefts, axis=1).astype(jnp.bfloat16)
    terms = jnp.dot(block, ladder[...], preferred_element_type=jnp.float32)
    high = terms.astype(jnp.bfloat16).astype(jnp.float32)
    rest = terms - high
    width = terms.shape[1]
    upper = jnp.concatenate(rights + [rest[:, : width // 2]], axis=1)
    lower = jnp.concatenate([high, rest[:, width // 2 :]], axis=1)
    out[...] = jnp.concatenate([upper, lower], axis=0).astype(jnp.bfloat16)
    tile = jnp.concatenate(
        [
            column_of(coupling[1:2, :]) * prev_right[...],
            column_of(coupling[0:1, :]) * prev_left[...],
        ],
        axis=1,
    )
    damped[...] = tile
    lane = lane_of((8, LANES))
    lack = jnp.sum(jnp.where(low, tile * swap(both[...]), 0.0), axis=1, keepdims=True)
    spread = jnp.where(lane == sublane_of((8, LANES)), lack, 0.0)
    missing[...] = jnp.sum(spread, axis=0, keepdims=True)


def right_kernel(turned, ladder, damped, missing, out):
    low = lane_of((8, LANES)) < HALF
    width = ladder.shape[1]
    block = turned[:, :width][:8]
    terms = lax.dot_general(
        block, ladder[...], (((1,), (1,)), ((), ())), preferred_element_type=jnp.float32
    )
    tiles = []
    for m in range(width // LANES):
        at = LANES * m
        side = at % (width // 2)
        half = 8 * (at // (width // 2))
        high = turned[:, at : at + LANES].astype(jnp.float32)[8:]
        rest = turned[:, width + side : width + side + LANES].astype(jnp.float32)[half : half + 8]
        left = high + rest
        piece = terms[:, at : at + LANES]
        tiles.append(jnp.where(low, piece, swap(left)))
        tiles.append(jnp.where(low, swap(piece), left))
    half = len(tiles) // 2
    near = lax.axis_index("chip") * lax.axis_size("core") + lax.axis_index("core")
    mine = lax.axis_index("far") * half + near
    own = damped[...]
    for at, tile in enumerate(tiles):
        tile = tile - jnp.where(mine == at, own, 0.0)
        for far in range(2):
            start = CHUNK * (far * half + at % half) + 8 * (at // half)
            out[start : start + 8, :] = tile
    for at in range(len(tiles)):
        out[CHUNK * at + 16 : CHUNK * at + 17, :] = missing[...]


def products_kernel(partials, gathered, rows, reduced):
    shape = (8, LANES)
    lane = lane_of(shape)
    low = lane < HALF
    count = gathered.shape[0]
    half = count // 2
    near = lax.axis_index("chip") * lax.axis_size("core") + lax.axis_index("core")
    mine = lax.axis_index("far")
    tiles = [0.0] * 6
    for far in range(2):
        pair = gathered[far * half + near]
        crossed = swap(pair)
        work = partials[8 * far : 8 * far + 8, :]
        for at in range(1, count):
            work = work + partials[CHUNK * at + 8 * far : CHUNK * at + 8 * far + 8, :]

        @pl.when(mine == far)
        def _(work=work):
            reduced[...] = work

        terms = (
            work * swap(work), work * crossed, pair * crossed, work * work,
            work * pair, pair * pair,
        )
        tiles = [tile + term for tile, term in zip(tiles, terms, strict=True)]
    cross, mixed, base_cross, square, own, base = tiles
    lack = partials[16:17, :]
    for at in range(1, count):
        lack = lack + partials[CHUNK * at + 16 : CHUNK * at + 17, :]

    def total(tile):
        return jnp.sum(tile, axis=1, keepdims=True)

    def lower(tile):
        return total(jnp.where(low, tile, 0.0))

    def upper(tile):
        return total(jnp.where(low, 0.0, tile))

    dots = (
        lower(mixed), lower(cross), total(mixed), lower(base_cross), lower(square),
        lower(own), lower(base), upper(square), upper(own), upper(base),
    )
    slot = lane // 8
    table = jnp.zeros(shape, jnp.float32)
    for at, dot in enumerate(dots):
        table = jnp.where(slot == at, dot, table)
    row = jnp.sum(jnp.where(lane % 8 == sublane_of(shape), table, 0.0), axis=0, keepdims=True)
    row = row + jnp.where(lane[:1] < 8, lack * (1.0 / half), 0.0)
    rows[...] = jnp.broadcast_to(row, rows.shape)


def finish_kernel(
    pairs_total, rows, reduced, both,
    next_right, next_left, coefficients, flag, right_here, left_here, coefficients_here, sems,
):
    shape = (8, LANES)
    lane = lane_of(shape)
    row = jnp.sum(rows[...], axis=0, keepdims=True) * (1.0 / pairs_total)
    wide = jnp.broadcast_to(row, shape)
    dots = [wide] + [pltpu.roll(wide, LANES - 8 * at, 1) for at in range(1, 10)]
    alpha = dots[0]
    square = alpha * alpha
    omega = dots[1] - alpha * dots[2] + square * dots[3]
    right_norm = dots[4] - 2.0 * alpha * dots[5] + square * dots[6]
    left_norm = dots[7] - 2.0 * alpha * dots[8] + square * dots[9]
    safe = jnp.maximum(
        jnp.abs(omega),
        0.1 * jnp.sqrt(jnp.maximum(right_norm, 0.0) * jnp.maximum(left_norm, 0.0) + 1e-6),
    )
    beta = jnp.sqrt(safe)
    gamma = omega / beta
    diagonal = lane == sublane_of(shape)

    def column(value):
        return jnp.sum(jnp.where(diagonal, value, 0.0), axis=1, keepdims=True)

    residual = reduced[...] - column(alpha) * both[...]
    scaled = residual * jnp.where(lane < HALF, column(1.0 / beta), column(gamma / safe))
    right_here[...] = scaled[:, :HALF]
    left_here[...] = scaled[:, HALF:]
    for at, value in enumerate((alpha, beta, gamma)):
        coefficients_here[at : at + 1, :] = value[:1, :8]
    targets = (next_right, next_left, coefficients)
    copies = fetch((right_here, left_here, coefficients_here), targets, sems)
    right_safe = right_norm - CANCEL * (dots[4] + square * dots[6])
    left_safe = left_norm - CANCEL * (dots[7] + square * dots[9])
    strong = jnp.minimum(right_safe, left_safe) > 0.0
    weak = jnp.where(jnp.logical_or(strong, lane >= 8), 0.0, 1.0)
    flag[0, 0] = jnp.max(weak).astype(jnp.int32)
    for copy in copies:
        copy.wait()


def direct(pairs_total, reduced, both, coefficients):
    alpha = coefficients[0]
    residual = reduced - alpha[:, None] * both
    right_res, left_res = residual[:, :HALF], residual[:, HALF:]
    sums = jnp.stack(
        [
            jnp.sum(left_res * right_res, axis=1),
            jnp.sum(right_res * right_res, axis=1),
            jnp.sum(left_res * left_res, axis=1),
        ]
    )
    omega, right_norm, left_norm = lax.psum(sums, AXES) / pairs_total
    safe = jnp.maximum(jnp.abs(omega), 0.1 * jnp.sqrt(right_norm * left_norm + 1e-6))
    beta = jnp.sqrt(safe)
    gamma = omega / beta
    next_right = right_res / beta[:, None]
    next_left = left_res * (gamma / safe)[:, None]
    return next_right, next_left, jnp.stack([alpha, beta, gamma])


def local(amplitudes_right, amplitudes_left, previous_right, previous_left, coupling, ladder):
    count = lax.axis_size(COL)
    devices = lax.axis_size(ROW) * count
    pairs_total = amplitudes_right.shape[1] * devices
    block = ladder.shape[1]
    folded = jax.ShapeDtypeStruct((16, block + block // 2), jnp.bfloat16)
    tile = jax.ShapeDtypeStruct((8, LANES), jnp.float32)
    ladder = pltpu.with_memory_space_constraint(ladder, pltpu.VMEM)

    half = pltpu.VMEM((8, HALF), jnp.float32)
    stay = functools.partial(pltpu.with_memory_space_constraint, memory_space=pltpu.HBM)
    wide = jax.ShapeDtypeStruct((count, 8, LANES), jnp.float32)
    with jax.named_scope("pack"):
        chunks, both = pl.pallas_call(
            pack_kernel, out_shape=(wide, tile), in_specs=[HBM] * 2, out_specs=(VMEM,) * 2,
            scratch_shapes=[half, half, pltpu.SemaphoreType.DMA((2,))],
            cost_estimate=pl.CostEstimate(
                flops=10_000_000_000, bytes_accessed=65_536, transcendentals=0
            ),
            compiler_params=PARAMS,
        )(stay(amplitudes_right), stay(amplitudes_left))
    gathered = lax.all_to_all(chunks, COL, 0, 0, tiled=True)
    with jax.named_scope("left_product"):
        packed, damped, missing = pl.pallas_call(
            left_kernel,
            out_shape=(folded, tile, jax.ShapeDtypeStruct((1, LANES), jnp.float32)),
            in_specs=[VMEM] * 6, out_specs=(VMEM,) * 3, compiler_params=PARAMS,
        )(gathered, ladder, both, previous_right, previous_left, coupling)
    transpose = [(i * count + j, j * count + i) for i in range(count) for j in range(count)]
    turned = lax.ppermute(packed, AXES, transpose)
    with jax.named_scope("right_product"):
        partials = pl.pallas_call(
            right_kernel, out_shape=jax.ShapeDtypeStruct((count * CHUNK, LANES), jnp.float32),
            in_specs=[VMEM] * 4, out_specs=VMEM, compiler_params=PARAMS,
        )(turned, ladder, damped, missing)
    partials = partials.reshape(count, CHUNK, 1, LANES)
    partials = lax.all_to_all(partials, COL, 0, 0, tiled=True).reshape(count * CHUNK, LANES)
    with jax.named_scope("inner_products"):
        rows, reduced = pl.pallas_call(
            products_kernel,
            out_shape=(tile, tile),
            in_specs=[VMEM] * 2, out_specs=(VMEM,) * 2, compiler_params=PARAMS,
        )(partials, gathered)
    other = lax.ppermute(rows, "core", ((0, 1), (1, 0)))
    with jax.named_scope("chip_total"):
        rows = jnp.broadcast_to((rows + other)[:1], (devices // 4, LANES))
    rows = lax.all_to_all(rows, ROW + COL[1:2], 0, 0, tiled=True)
    half_out = pltpu.HBM((8, HALF), jnp.float32)
    with jax.named_scope("finish"):
        next_right, next_left, coefficients, flag = pl.pallas_call(
            functools.partial(finish_kernel, float(pairs_total)),
            out_shape=(
                half_out, half_out, pltpu.HBM((3, 8), jnp.float32),
                pltpu.SMEM((1, 1), jnp.int32),
            ),
            in_specs=[VMEM] * 3,
            out_specs=(HBM,) * 3 + (pl.BlockSpec(memory_space=pltpu.SMEM),),
            scratch_shapes=[
                half, half, pltpu.VMEM((3, 8), jnp.float32), pltpu.SemaphoreType.DMA((3,)),
            ],
            compiler_params=PARAMS,
        )(rows, reduced, both)
    return lax.cond(
        flag[0, 0] > 0,
        lambda: direct(float(pairs_total), reduced, both, coefficients),
        lambda: (next_right, next_left, coefficients),
    )


def solution(mesh):
    rows_count, cols_count = mesh.devices.shape
    mesh = jax.sharding.Mesh(mesh.devices.reshape(rows_count, 2, cols_count // 4, 2), ROW + COL)
    placed = (
        P(None, AXES),
        P(None, AXES),
        P(None, AXES),
        P(None, AXES),
        P(),
        P(ROW, COL),
    )
    return jax.shard_map(
        local,
        mesh=mesh,
        in_specs=placed,
        out_specs=(P(None, AXES), P(None, AXES), P()),
        check_vma=False,
    )
```

```python
import functools

import jax
import jax.numpy as jnp
from jax import lax
from jax.experimental import pallas as pl
from jax.experimental.pallas import tpu as pltpu
from jax.sharding import PartitionSpec as P

ROW = ("row",)
COL = ("far", "chip", "core")
AXES = ROW + COL
HALF = 64
LANES = 128
CHUNK = 17
CANCEL = 1e-3
VMEM = pl.BlockSpec(memory_space=pltpu.VMEM)
HBM = pl.BlockSpec(memory_space=pltpu.HBM)
PARAMS = pltpu.CompilerParams(vmem_limit_bytes=32 * 1024 * 1024)


def lane_of(shape):
    return lax.broadcasted_iota(jnp.int32, shape, 1)


def sublane_of(shape):
    return lax.broadcasted_iota(jnp.int32, shape, 0)


def swap(tile):
    return pltpu.roll(tile, HALF, 1)


def column_of(row):
    wide = jnp.broadcast_to(row, (8, 8))
    return jnp.sum(jnp.where(lane_of((8, 8)) == sublane_of((8, 8)), wide, 0.0), axis=1, keepdims=True)


def fetch(sources, targets, sems):
    copies = [
        pltpu.make_async_copy(source, target, sems.at[at])
        for at, (source, target) in enumerate(zip(sources, targets, strict=True))
    ]
    for copy in copies:
        copy.start()
    return copies


def pack_kernel(right, left, chunks, both, right_here, left_here, sems):
    for copy in fetch((right, left), (right_here, left_here), sems):
        copy.wait()
    tile = jnp.concatenate([right_here[...], left_here[...]], axis=1)
    both[...] = tile
    chunks[...] = jnp.broadcast_to(tile[None], chunks.shape)


def left_kernel(
    gathered, ladder, both, prev_right, prev_left, coupling, out, damped, missing
):
    low = lane_of((8, LANES)) < HALF
    rights, lefts = [], []
    for m in range(gathered.shape[0] // 2):
        even, odd = gathered[2 * m], gathered[2 * m + 1]
        rights.append(jnp.where(low, even, swap(odd)))
        lefts.append(jnp.where(low, swap(even), odd))
    block = jnp.concatenate(lefts, axis=1).astype(jnp.bfloat16)
    terms = jnp.dot(block, ladder[...], preferred_element_type=jnp.float32)
    high = terms.astype(jnp.bfloat16).astype(jnp.float32)
    rest = terms - high
    width = terms.shape[1]
    upper = jnp.concatenate(rights + [rest[:, : width // 2]], axis=1)
    lower = jnp.concatenate([high, rest[:, width // 2 :]], axis=1)
    out[...] = jnp.concatenate([upper, lower], axis=0).astype(jnp.bfloat16)
    tile = jnp.concatenate(
        [
            column_of(coupling[1:2, :]) * prev_right[...],
            column_of(coupling[0:1, :]) * prev_left[...],
        ],
        axis=1,
    )
    damped[...] = tile
    lane = lane_of((8, LANES))
    lack = jnp.sum(jnp.where(low, tile * swap(both[...]), 0.0), axis=1, keepdims=True)
    spread = jnp.where(lane == sublane_of((8, LANES)), lack, 0.0)
    missing[...] = jnp.sum(spread, axis=0, keepdims=True)


def flip_kernel(ladder, damped, flipped):
    del damped
    flipped[...] = ladder[...].T


def right_kernel(turned, ladder, damped, missing, out):
    low = lane_of((8, LANES)) < HALF
    width = ladder.shape[1]
    block = turned[:, :width][:8]
    terms = jnp.dot(block, ladder[...], preferred_element_type=jnp.float32)
    tiles = []
    for m in range(width // LANES):
        at = LANES * m
        side = at % (width // 2)
        half = 8 * (at // (width // 2))
        high = turned[:, at : at + LANES].astype(jnp.float32)[8:]
        rest = turned[:, width + side : width + side + LANES].astype(jnp.float32)[half : half + 8]
        left = high + rest
        piece = terms[:, at : at + LANES]
        tiles.append(jnp.where(low, piece, swap(left)))
        tiles.append(jnp.where(low, swap(piece), left))
    half = len(tiles) // 2
    near = lax.axis_index("chip") * lax.axis_size("core") + lax.axis_index("core")
    mine = lax.axis_index("far") * half + near
    own = damped[...]
    for at, tile in enumerate(tiles):
        tile = tile - jnp.where(mine == at, own, 0.0)
        for far in range(2):
            start = CHUNK * (far * half + at % half) + 8 * (at // half)
            out[start : start + 8, :] = tile
    for at in range(len(tiles)):
        out[CHUNK * at + 16 : CHUNK * at + 17, :] = missing[...]


def products_kernel(partials, gathered, rows, reduced):
    shape = (8, LANES)
    lane = lane_of(shape)
    low = lane < HALF
    count = gathered.shape[0]
    half = count // 2
    near = lax.axis_index("chip") * lax.axis_size("core") + lax.axis_index("core")
    mine = lax.axis_index("far")
    tiles = [0.0] * 6
    for far in range(2):
        pair = gathered[far * half + near]
        crossed = swap(pair)
        work = partials[8 * far : 8 * far + 8, :]
        for at in range(1, count):
            work = work + partials[CHUNK * at + 8 * far : CHUNK * at + 8 * far + 8, :]

        @pl.when(mine == far)
        def _(work=work):
            reduced[...] = work

        terms = (
            work * swap(work), work * crossed, pair * crossed, work * work,
            work * pair, pair * pair,
        )
        tiles = [tile + term for tile, term in zip(tiles, terms, strict=True)]
    cross, mixed, base_cross, square, own, base = tiles
    lack = partials[16:17, :]
    for at in range(1, count):
        lack = lack + partials[CHUNK * at + 16 : CHUNK * at + 17, :]

    def total(tile):
        return jnp.sum(tile, axis=1, keepdims=True)

    def lower(tile):
        return total(jnp.where(low, tile, 0.0))

    def upper(tile):
        return total(jnp.where(low, 0.0, tile))

    dots = (
        lower(mixed), lower(cross), total(mixed), lower(base_cross), lower(square),
        lower(own), lower(base), upper(square), upper(own), upper(base),
    )
    slot = lane // 8
    table = jnp.zeros(shape, jnp.float32)
    for at, dot in enumerate(dots):
        table = jnp.where(slot == at, dot, table)
    row = jnp.sum(jnp.where(lane % 8 == sublane_of(shape), table, 0.0), axis=0, keepdims=True)
    row = row + jnp.where(lane[:1] < 8, lack * (1.0 / half), 0.0)
    rows[...] = jnp.broadcast_to(row, rows.shape)


def finish_kernel(
    pairs_total, rows, reduced, both,
    next_right, next_left, coefficients, flag, right_here, left_here, coefficients_here, sems,
):
    shape = (8, LANES)
    lane = lane_of(shape)
    row = jnp.sum(rows[...], axis=0, keepdims=True) * (1.0 / pairs_total)
    wide = jnp.broadcast_to(row, shape)
    dots = [wide] + [pltpu.roll(wide, LANES - 8 * at, 1) for at in range(1, 10)]
    alpha = dots[0]
    square = alpha * alpha
    omega = dots[1] - alpha * dots[2] + square * dots[3]
    right_norm = dots[4] - 2.0 * alpha * dots[5] + square * dots[6]
    left_norm = dots[7] - 2.0 * alpha * dots[8] + square * dots[9]
    safe = jnp.maximum(
        jnp.abs(omega),
        0.1 * jnp.sqrt(jnp.maximum(right_norm, 0.0) * jnp.maximum(left_norm, 0.0) + 1e-6),
    )
    beta = jnp.sqrt(safe)
    gamma = omega / beta
    diagonal = lane == sublane_of(shape)

    def column(value):
        return jnp.sum(jnp.where(diagonal, value, 0.0), axis=1, keepdims=True)

    residual = reduced[...] - column(alpha) * both[...]
    scaled = residual * jnp.where(lane < HALF, column(1.0 / beta), column(gamma / safe))
    right_here[...] = scaled[:, :HALF]
    left_here[...] = scaled[:, HALF:]
    for at, value in enumerate((alpha, beta, gamma)):
        coefficients_here[at : at + 1, :] = value[:1, :8]
    targets = (next_right, next_left, coefficients)
    copies = fetch((right_here, left_here, coefficients_here), targets, sems)
    right_safe = right_norm - CANCEL * (dots[4] + square * dots[6])
    left_safe = left_norm - CANCEL * (dots[7] + square * dots[9])
    strong = jnp.minimum(right_safe, left_safe) > 0.0
    weak = jnp.where(jnp.logical_or(strong, lane >= 8), 0.0, 1.0)
    flag[0, 0] = jnp.max(weak).astype(jnp.int32)
    for copy in copies:
        copy.wait()


def direct(pairs_total, reduced, both, coefficients):
    alpha = coefficients[0]
    residual = reduced - alpha[:, None] * both
    right_res, left_res = residual[:, :HALF], residual[:, HALF:]
    sums = jnp.stack(
        [
            jnp.sum(left_res * right_res, axis=1),
            jnp.sum(right_res * right_res, axis=1),
            jnp.sum(left_res * left_res, axis=1),
        ]
    )
    omega, right_norm, left_norm = lax.psum(sums, AXES) / pairs_total
    safe = jnp.maximum(jnp.abs(omega), 0.1 * jnp.sqrt(right_norm * left_norm + 1e-6))
    beta = jnp.sqrt(safe)
    gamma = omega / beta
    next_right = right_res / beta[:, None]
    next_left = left_res * (gamma / safe)[:, None]
    return next_right, next_left, jnp.stack([alpha, beta, gamma])


def local(amplitudes_right, amplitudes_left, previous_right, previous_left, coupling, ladder):
    count = lax.axis_size(COL)
    devices = lax.axis_size(ROW) * count
    pairs_total = amplitudes_right.shape[1] * devices
    block = ladder.shape[1]
    folded = jax.ShapeDtypeStruct((16, block + block // 2), jnp.bfloat16)
    tile = jax.ShapeDtypeStruct((8, LANES), jnp.float32)
    ladder = pltpu.with_memory_space_constraint(ladder, pltpu.VMEM)

    half = pltpu.VMEM((8, HALF), jnp.float32)
    stay = functools.partial(pltpu.with_memory_space_constraint, memory_space=pltpu.HBM)
    wide = jax.ShapeDtypeStruct((count, 8, LANES), jnp.float32)
    with jax.named_scope("pack"):
        chunks, both = pl.pallas_call(
            pack_kernel, out_shape=(wide, tile), in_specs=[HBM] * 2, out_specs=(VMEM,) * 2,
            scratch_shapes=[half, half, pltpu.SemaphoreType.DMA((2,))],
            cost_estimate=pl.CostEstimate(
                flops=10_000_000_000, bytes_accessed=65_536, transcendentals=0
            ),
            compiler_params=PARAMS,
        )(stay(amplitudes_right), stay(amplitudes_left))
    gathered = lax.all_to_all(chunks, COL, 0, 0, tiled=True)
    with jax.named_scope("left_product"):
        packed, damped, missing = pl.pallas_call(
            left_kernel,
            out_shape=(folded, tile, jax.ShapeDtypeStruct((1, LANES), jnp.float32)),
            in_specs=[VMEM] * 6, out_specs=(VMEM,) * 3, compiler_params=PARAMS,
        )(gathered, ladder, both, previous_right, previous_left, coupling)
    transpose = [(i * count + j, j * count + i) for i in range(count) for j in range(count)]
    turned = lax.ppermute(packed, AXES, transpose)
    with jax.named_scope("flip"):
        flipped = pl.pallas_call(
            flip_kernel, out_shape=jax.ShapeDtypeStruct(ladder.shape[::-1], ladder.dtype),
            in_specs=[VMEM] * 2, out_specs=VMEM, compiler_params=PARAMS,
            cost_estimate=pl.CostEstimate(
                flops=1_000_000_000, bytes_accessed=4_194_304, transcendentals=0
            ),
        )(ladder, damped)
    with jax.named_scope("right_product"):
        partials = pl.pallas_call(
            right_kernel, out_shape=jax.ShapeDtypeStruct((count * CHUNK, LANES), jnp.float32),
            in_specs=[VMEM] * 4, out_specs=VMEM, compiler_params=PARAMS,
        )(turned, flipped, damped, missing)
    partials = partials.reshape(count, CHUNK, 1, LANES)
    partials = lax.all_to_all(partials, COL, 0, 0, tiled=True).reshape(count * CHUNK, LANES)
    with jax.named_scope("inner_products"):
        rows, reduced = pl.pallas_call(
            products_kernel,
            out_shape=(tile, tile),
            in_specs=[VMEM] * 2, out_specs=(VMEM,) * 2, compiler_params=PARAMS,
        )(partials, gathered)
    other = lax.ppermute(rows, "core", ((0, 1), (1, 0)))
    with jax.named_scope("chip_total"):
        rows = jnp.broadcast_to((rows + other)[:1], (devices // 4, LANES))
    rows = lax.all_to_all(rows, ROW + COL[1:2], 0, 0, tiled=True)
    half_out = pltpu.HBM((8, HALF), jnp.float32)
    with jax.named_scope("finish"):
        next_right, next_left, coefficients, flag = pl.pallas_call(
            functools.partial(finish_kernel, float(pairs_total)),
            out_shape=(
                half_out, half_out, pltpu.HBM((3, 8), jnp.float32),
                pltpu.SMEM((1, 1), jnp.int32),
            ),
            in_specs=[VMEM] * 3,
            out_specs=(HBM,) * 3 + (pl.BlockSpec(memory_space=pltpu.SMEM),),
            scratch_shapes=[
                half, half, pltpu.VMEM((3, 8), jnp.float32), pltpu.SemaphoreType.DMA((3,)),
            ],
            compiler_params=PARAMS,
        )(rows, reduced, both)
    return lax.cond(
        flag[0, 0] > 0,
        lambda: direct(float(pairs_total), reduced, both, coefficients),
        lambda: (next_right, next_left, coefficients),
    )


def solution(mesh):
    rows_count, cols_count = mesh.devices.shape
    mesh = jax.sharding.Mesh(mesh.devices.reshape(rows_count, 2, cols_count // 4, 2), ROW + COL)
    placed = (
        P(None, AXES),
        P(None, AXES),
        P(None, AXES),
        P(None, AXES),
        P(),
        P(ROW, COL),
    )
    return jax.shard_map(
        local,
        mesh=mesh,
        in_specs=placed,
        out_specs=(P(None, AXES), P(None, AXES), P()),
        check_vma=False,
    )
```

```python
import functools

import jax
import jax.numpy as jnp
from jax import lax
from jax.experimental import pallas as pl
from jax.experimental.pallas import tpu as pltpu
from jax.sharding import PartitionSpec as P

ROW = ("row",)
COL = ("far", "chip", "core")
AXES = ROW + COL
HALF = 64
LANES = 128
CHUNK = 17
CANCEL = 1e-3
VMEM = pl.BlockSpec(memory_space=pltpu.VMEM)
HBM = pl.BlockSpec(memory_space=pltpu.HBM)
PARAMS = pltpu.CompilerParams(vmem_limit_bytes=32 * 1024 * 1024)


def lane_of(shape):
    return lax.broadcasted_iota(jnp.int32, shape, 1)


def sublane_of(shape):
    return lax.broadcasted_iota(jnp.int32, shape, 0)


def swap(tile):
    return pltpu.roll(tile, HALF, 1)


def column_of(row):
    wide = jnp.broadcast_to(row, (8, 8))
    return jnp.sum(jnp.where(lane_of((8, 8)) == sublane_of((8, 8)), wide, 0.0), axis=1, keepdims=True)


def fetch(sources, targets, sems):
    copies = [
        pltpu.make_async_copy(source, target, sems.at[at])
        for at, (source, target) in enumerate(zip(sources, targets, strict=True))
    ]
    for copy in copies:
        copy.start()
    return copies


def pack_kernel(right, left, chunks, both, right_here, left_here, sems):
    for copy in fetch((right, left), (right_here, left_here), sems):
        copy.wait()
    tile = jnp.concatenate([right_here[...], left_here[...]], axis=1)
    both[...] = tile
    chunks[...] = jnp.broadcast_to(tile[None], chunks.shape)


def left_kernel(
    gathered, ladder, both, prev_right, prev_left, coupling, out, damped, missing
):
    low = lane_of((8, LANES)) < HALF
    rights, lefts = [], []
    for m in range(gathered.shape[0] // 2):
        even, odd = gathered[2 * m], gathered[2 * m + 1]
        rights.append(jnp.where(low, even, swap(odd)))
        lefts.append(jnp.where(low, swap(even), odd))
    block = jnp.concatenate(lefts, axis=1).astype(jnp.bfloat16)
    terms = jnp.dot(block, ladder[...], preferred_element_type=jnp.float32)
    high = terms.astype(jnp.bfloat16).astype(jnp.float32)
    rest = terms - high
    width = terms.shape[1]
    upper = jnp.concatenate(rights + [rest[:, : width // 2]], axis=1)
    lower = jnp.concatenate([high, rest[:, width // 2 :]], axis=1)
    out[...] = jnp.concatenate([upper, lower], axis=0).astype(jnp.bfloat16)
    tile = jnp.concatenate(
        [
            column_of(coupling[1:2, :]) * prev_right[...],
            column_of(coupling[0:1, :]) * prev_left[...],
        ],
        axis=1,
    )
    damped[...] = tile
    lane = lane_of((8, LANES))
    lack = jnp.sum(jnp.where(low, tile * swap(both[...]), 0.0), axis=1, keepdims=True)
    spread = jnp.where(lane == sublane_of((8, LANES)), lack, 0.0)
    missing[...] = jnp.sum(spread, axis=0, keepdims=True)


def flip_kernel(ladder, damped, flipped):
    del damped
    flipped[...] = ladder[...].T


def right_kernel(turned, ladder, damped, missing, out):
    low = lane_of((8, LANES)) < HALF
    width = ladder.shape[1]
    block = turned[:, :width][:8]
    terms = jnp.dot(block, ladder[...], preferred_element_type=jnp.float32)
    tiles = []
    for m in range(width // LANES):
        at = LANES * m
        side = at % (width // 2)
        half = 8 * (at // (width // 2))
        high = turned[:, at : at + LANES].astype(jnp.float32)[8:]
        rest = turned[:, width + side : width + side + LANES].astype(jnp.float32)[half : half + 8]
        left = high + rest
        piece = terms[:, at : at + LANES]
        tiles.append(jnp.where(low, piece, swap(left)))
        tiles.append(jnp.where(low, swap(piece), left))
    half = len(tiles) // 2
    near = lax.axis_index("chip") * lax.axis_size("core") + lax.axis_index("core")
    mine = lax.axis_index("far") * half + near
    own = damped[...]
    for at, tile in enumerate(tiles):
        tile = tile - jnp.where(mine == at, own, 0.0)
        for far in range(2):
            start = CHUNK * (far * half + at % half) + 8 * (at // half)
            out[start : start + 8, :] = tile
    for at in range(len(tiles)):
        out[CHUNK * at + 16 : CHUNK * at + 17, :] = missing[...]


def products_kernel(partials, gathered, rows, reduced):
    shape = (8, LANES)
    lane = lane_of(shape)
    low = lane < HALF
    count = gathered.shape[0]
    half = count // 2
    near = lax.axis_index("chip") * lax.axis_size("core") + lax.axis_index("core")
    mine = lax.axis_index("far")
    tiles = [0.0] * 6
    for far in range(2):
        pair = gathered[far * half + near]
        crossed = swap(pair)
        parts = [
            partials[CHUNK * at + 8 * far : CHUNK * at + 8 * far + 8, :] for at in range(count)
        ]
        while len(parts) > 1:
            parts = [first + second for first, second in zip(parts[::2], parts[1::2], strict=True)]
        work = parts[0]

        @pl.when(mine == far)
        def _(work=work):
            reduced[...] = work

        terms = (
            work * swap(work), work * crossed, pair * crossed, work * work,
            work * pair, pair * pair,
        )
        tiles = [tile + term for tile, term in zip(tiles, terms, strict=True)]
    cross, mixed, base_cross, square, own, base = tiles
    lack = partials[16:17, :]
    for at in range(1, count):
        lack = lack + partials[CHUNK * at + 16 : CHUNK * at + 17, :]

    def total(tile):
        return jnp.sum(tile, axis=1, keepdims=True)

    def lower(tile):
        return total(jnp.where(low, tile, 0.0))

    def upper(tile):
        return total(jnp.where(low, 0.0, tile))

    dots = (
        lower(mixed), lower(cross), total(mixed), lower(base_cross), lower(square),
        lower(own), lower(base), upper(square), upper(own), upper(base),
    )
    slot = lane // 8
    table = jnp.zeros(shape, jnp.float32)
    for at, dot in enumerate(dots):
        table = jnp.where(slot == at, dot, table)
    row = jnp.sum(jnp.where(lane % 8 == sublane_of(shape), table, 0.0), axis=0, keepdims=True)
    row = row + jnp.where(lane[:1] < 8, lack * (1.0 / half), 0.0)
    rows[...] = row


def finish_kernel(
    pairs_total, rows, reduced, both,
    next_right, next_left, coefficients, flag, right_here, left_here, coefficients_here, sems,
):
    shape = (8, LANES)
    lane = lane_of(shape)
    row = jnp.sum(rows[...], axis=0, keepdims=True) * (1.0 / pairs_total)
    wide = jnp.broadcast_to(row, shape)
    dots = [wide] + [pltpu.roll(wide, LANES - 8 * at, 1) for at in range(1, 10)]
    alpha = dots[0]
    square = alpha * alpha
    omega = dots[1] - alpha * dots[2] + square * dots[3]
    right_norm = dots[4] - 2.0 * alpha * dots[5] + square * dots[6]
    left_norm = dots[7] - 2.0 * alpha * dots[8] + square * dots[9]
    safe = jnp.maximum(
        jnp.abs(omega),
        0.1 * jnp.sqrt(jnp.maximum(right_norm, 0.0) * jnp.maximum(left_norm, 0.0) + 1e-6),
    )
    beta = jnp.sqrt(safe)
    gamma = omega / beta
    diagonal = lane == sublane_of(shape)

    def column(value):
        return jnp.sum(jnp.where(diagonal, value, 0.0), axis=1, keepdims=True)

    residual = reduced[...] - column(alpha) * both[...]
    scaled = residual * jnp.where(lane < HALF, column(1.0 / beta), column(gamma / safe))
    right_here[...] = scaled[:, :HALF]
    left_here[...] = scaled[:, HALF:]
    for at, value in enumerate((alpha, beta, gamma)):
        coefficients_here[at : at + 1, :] = value[:1, :8]
    targets = (next_right, next_left, coefficients)
    copies = fetch((right_here, left_here, coefficients_here), targets, sems)
    right_safe = right_norm - CANCEL * (dots[4] + square * dots[6])
    left_safe = left_norm - CANCEL * (dots[7] + square * dots[9])
    strong = jnp.minimum(right_safe, left_safe) > 0.0
    weak = jnp.where(jnp.logical_or(strong, lane >= 8), 0.0, 1.0)
    flag[0, 0] = jnp.max(weak).astype(jnp.int32)
    for copy in copies:
        copy.wait()


def direct(pairs_total, reduced, both, coefficients):
    alpha = coefficients[0]
    residual = reduced - alpha[:, None] * both
    right_res, left_res = residual[:, :HALF], residual[:, HALF:]
    sums = jnp.stack(
        [
            jnp.sum(left_res * right_res, axis=1),
            jnp.sum(right_res * right_res, axis=1),
            jnp.sum(left_res * left_res, axis=1),
        ]
    )
    omega, right_norm, left_norm = lax.psum(sums, AXES) / pairs_total
    safe = jnp.maximum(jnp.abs(omega), 0.1 * jnp.sqrt(right_norm * left_norm + 1e-6))
    beta = jnp.sqrt(safe)
    gamma = omega / beta
    next_right = right_res / beta[:, None]
    next_left = left_res * (gamma / safe)[:, None]
    return next_right, next_left, jnp.stack([alpha, beta, gamma])


def local(amplitudes_right, amplitudes_left, previous_right, previous_left, coupling, ladder):
    count = lax.axis_size(COL)
    devices = lax.axis_size(ROW) * count
    pairs_total = amplitudes_right.shape[1] * devices
    block = ladder.shape[1]
    folded = jax.ShapeDtypeStruct((16, block + block // 2), jnp.bfloat16)
    tile = jax.ShapeDtypeStruct((8, LANES), jnp.float32)
    ladder = pltpu.with_memory_space_constraint(ladder, pltpu.VMEM)

    half = pltpu.VMEM((8, HALF), jnp.float32)
    stay = functools.partial(pltpu.with_memory_space_constraint, memory_space=pltpu.HBM)
    wide = jax.ShapeDtypeStruct((count, 8, LANES), jnp.float32)
    with jax.named_scope("pack"):
        chunks, both = pl.pallas_call(
            pack_kernel, out_shape=(wide, tile), in_specs=[HBM] * 2, out_specs=(VMEM,) * 2,
            scratch_shapes=[half, half, pltpu.SemaphoreType.DMA((2,))],
            cost_estimate=pl.CostEstimate(
                flops=10_000_000_000, bytes_accessed=65_536, transcendentals=0
            ),
            compiler_params=PARAMS,
        )(stay(amplitudes_right), stay(amplitudes_left))
    gathered = lax.all_to_all(chunks, COL, 0, 0, tiled=True)
    with jax.named_scope("left_product"):
        packed, damped, missing = pl.pallas_call(
            left_kernel,
            out_shape=(folded, tile, jax.ShapeDtypeStruct((1, LANES), jnp.float32)),
            in_specs=[VMEM] * 6, out_specs=(VMEM,) * 3, compiler_params=PARAMS,
        )(gathered, ladder, both, previous_right, previous_left, coupling)
    transpose = [(i * count + j, j * count + i) for i in range(count) for j in range(count)]
    turned = lax.ppermute(packed, AXES, transpose)
    with jax.named_scope("flip"):
        flipped = pl.pallas_call(
            flip_kernel, out_shape=jax.ShapeDtypeStruct(ladder.shape[::-1], ladder.dtype),
            in_specs=[VMEM] * 2, out_specs=VMEM, compiler_params=PARAMS,
            cost_estimate=pl.CostEstimate(
                flops=1_000_000_000, bytes_accessed=4_194_304, transcendentals=0
            ),
        )(ladder, damped)
    with jax.named_scope("right_product"):
        partials = pl.pallas_call(
            right_kernel, out_shape=jax.ShapeDtypeStruct((count * CHUNK, LANES), jnp.float32),
            in_specs=[VMEM] * 4, out_specs=VMEM, compiler_params=PARAMS,
        )(turned, flipped, damped, missing)
    partials = partials.reshape(count, CHUNK, 1, LANES)
    partials = lax.all_to_all(partials, COL, 0, 0, tiled=True).reshape(count * CHUNK, LANES)
    with jax.named_scope("inner_products"):
        rows, reduced = pl.pallas_call(
            products_kernel,
            out_shape=(jax.ShapeDtypeStruct((1, LANES), jnp.float32), tile),
            in_specs=[VMEM] * 2, out_specs=(VMEM,) * 2, compiler_params=PARAMS,
        )(partials, gathered)
    other = lax.ppermute(rows, "core", ((0, 1), (1, 0)))
    with jax.named_scope("chip_total"):
        rows = jnp.broadcast_to(rows + other, (devices // 4, LANES))
    rows = lax.all_to_all(rows, ROW + COL[1:2], 0, 0, tiled=True)
    half_out = pltpu.HBM((8, HALF), jnp.float32)
    with jax.named_scope("finish"):
        next_right, next_left, coefficients, flag = pl.pallas_call(
            functools.partial(finish_kernel, float(pairs_total)),
            out_shape=(
                half_out, half_out, pltpu.HBM((3, 8), jnp.float32),
                pltpu.SMEM((1, 1), jnp.int32),
            ),
            in_specs=[VMEM] * 3,
            out_specs=(HBM,) * 3 + (pl.BlockSpec(memory_space=pltpu.SMEM),),
            scratch_shapes=[
                half, half, pltpu.VMEM((3, 8), jnp.float32), pltpu.SemaphoreType.DMA((3,)),
            ],
            compiler_params=PARAMS,
        )(rows, reduced, both)
    return lax.cond(
        flag[0, 0] > 0,
        lambda: direct(float(pairs_total), reduced, both, coefficients),
        lambda: (next_right, next_left, coefficients),
    )


def solution(mesh):
    rows_count, cols_count = mesh.devices.shape
    mesh = jax.sharding.Mesh(mesh.devices.reshape(rows_count, 2, cols_count // 4, 2), ROW + COL)
    placed = (
        P(None, AXES),
        P(None, AXES),
        P(None, AXES),
        P(None, AXES),
        P(),
        P(ROW, COL),
    )
    return jax.shard_map(
        local,
        mesh=mesh,
        in_specs=placed,
        out_specs=(P(None, AXES), P(None, AXES), P()),
        check_vma=False,
    )
```
